32 devices in a mesh: img: 8 (over z, y), cap: 4 (over x, core).
Axes of the slice: x: 2, y: 2, z: 4, core: 2. Of those that a mesh axis runs over, the one named last changes fastest.
Arguments:
- pair_list: int32 [512, 2], replicated, may hold values from 0 to 127, as said below
- verify_order: int32 [512], P(('img', 'cap')), may hold values from 0 to 511, as said below
- image_slot: int32 [64], replicated, may hold values from 0 to 63, as said below
- caption_slot: int32 [128], replicated, may hold values from 0 to 127, as said below
- images: bfloat16 [64, 197, 768], P('img'), may hold values from -6 to 6
- captions: bfloat16 [128, 32, 768], P('cap'), may hold values from -6 to 6
- query_weight: bfloat16 [768, 768], replicated, may hold values from -1 to 1
- key_weight: bfloat16 [768, 768], replicated, may hold values from -1 to 1
- value_weight: bfloat16 [768, 768], replicated, may hold values from -0.21875 to 0.21875
- out_weight: bfloat16 [768, 768], replicated, may hold values from -0.4375 to 0.4375
- gain_attn: float32 [768], replicated, may hold values from 0.5 to 1.5
- in_weight: bfloat16 [768, 3072], replicated, may hold values from -0.21875 to 0.21875
- back_weight: bfloat16 [3072, 768], replicated, may hold values from -0.109375 to 0.109375
- gain_ffn: float32 [768], replicated, may hold values from 0.5 to 1.5
- match_weight: bfloat16 [768, 2], replicated, may hold values from -0.21875 to 0.21875
Outputs:
- merged: bfloat16 [512, 32, 768], P(('img', 'cap'))
- match_logits: float32 [512, 2], P(('img', 'cap'))
The draws below stay inside these ranges and needn't reach their ends.
Inputs may be any that keep to these rules, and one draw needn't show every extreme that they name: Each image id and caption id of pair_list lies in range; image_slot is a permutation. caption_slot is a permutation. verify_order is a permutation. Of the 16 rows verified by one device, at most 2 have images stored on one index of img and at most 4 have captions stored on one index of cap; every device has some index reaching each bound. `pair_list`: column 0 holds image ids, column 1 caption ids.
All inputs are finite; a program needn't handle non-finite values.
Results may differ from the reference program's by a relative error of at most 0.018.
Values may be sent and summed in bfloat16 or wider, within the bound.
No kernel may reach another device: no remote copies, remote signals or barrier semaphores. Data moves between devices by JAX's collectives and lax.ppermute only.
A program may use at most 192 MiB of HBM per device.

```python
import jax
import jax.numpy as jnp
from jax import lax

D = 768
HEADS = 12
FF = 3072
LP = 197
LCAP = 32
PAIR_DEV = 16
IMG_DEV = 8
CAP_DEV = 32
IMG_MOST = 2
CAP_MOST = 4
NIMG = 64
NCAP = 128
PAIRS = 512


def owner_rows(key, owner_count, capacity, rows_dev):
    slot_count = owner_count * capacity
    first_key, second_key, third_key = jax.random.split(key, 3)
    ranks = jax.random.permutation(first_key, slot_count).astype(jnp.int32)
    chosen_owner = jax.random.randint(second_key, (), 0, owner_count)
    slot_owner = jnp.arange(slot_count, dtype=jnp.int32) // capacity
    ranks = jnp.where(slot_owner == chosen_owner, ranks - slot_count, ranks)
    picked = jnp.argsort(ranks)[:rows_dev]
    picked = jax.random.permutation(third_key, picked)
    return (picked // capacity).astype(jnp.int32)


def build_all(key):
    n_img = NIMG // IMG_DEV
    n_cap = NCAP // CAP_DEV
    device_count = PAIRS // PAIR_DEV
    keys = [jax.random.fold_in(key, 7001 + number) for number in range(8)]
    image_slot = jax.random.permutation(keys[0], NIMG).astype(jnp.int32)
    caption_slot = jax.random.permutation(keys[1], NCAP).astype(jnp.int32)
    image_inverse = jnp.zeros((NIMG,), jnp.int32).at[image_slot].set(jnp.arange(NIMG, dtype=jnp.int32))
    caption_inverse = jnp.zeros((NCAP,), jnp.int32).at[caption_slot].set(jnp.arange(NCAP, dtype=jnp.int32))
    image_owner = jax.vmap(lambda k: owner_rows(k, n_img, IMG_MOST, PAIR_DEV))(jax.random.split(keys[2], device_count)).reshape(-1)
    caption_owner = jax.vmap(lambda k: owner_rows(k, n_cap, CAP_MOST, PAIR_DEV))(jax.random.split(keys[3], device_count)).reshape(-1)
    image_store = image_owner * IMG_DEV + jax.random.randint(keys[4], (PAIRS,), 0, IMG_DEV)
    caption_store = caption_owner * CAP_DEV + jax.random.randint(keys[5], (PAIRS,), 0, CAP_DEV)
    pair_rows = jnp.stack([jnp.take(image_inverse, image_store), jnp.take(caption_inverse, caption_store)], axis=1).astype(jnp.int32)
    verify_order = jax.random.permutation(keys[6], PAIRS).astype(jnp.int32)
    pair_list = jnp.zeros((PAIRS, 2), jnp.int32).at[verify_order].set(pair_rows)
    return (pair_list, verify_order, image_slot, caption_slot)


def draw_pair_list(key, part):
    return build_all(key)[0]


def draw_verify_order(key, part):
    return build_all(key)[1]


def draw_image_slot(key, part):
    return build_all(key)[2]


def draw_caption_slot(key, part):
    return build_all(key)[3]


def shared_direction(key):
    return jnp.clip(jax.random.normal(jax.random.fold_in(key, 9101), (D,), jnp.float32), -2.0, 2.0)


def planted_rows(key, base_key, noise, chance, lowest, highest):
    row_shape = noise.shape[:-1] + (1,)
    planted = jax.random.bernoulli(jax.random.fold_in(key, 2), chance, row_shape)
    strength = jax.random.uniform(jax.random.fold_in(key, 3), row_shape, jnp.float32, lowest, highest)
    rows = noise + jnp.where(planted, strength, 0.0) * shared_direction(base_key)
    return jnp.clip(rows, -6.0, 6.0)


def draw_images(key, part):
    own_key = jax.random.fold_in(key, 9301)
    noise_key = jax.random.fold_in(own_key, 1)
    noise = jnp.clip(jax.random.normal(noise_key, (NIMG, LP, D), jnp.float32), -4.0, 4.0)
    return planted_rows(own_key, key, noise, min(8.0 / LP, 0.5), 0.5, 3.5).astype(jnp.bfloat16)


def draw_captions(key, part):
    own_key = jax.random.fold_in(key, 9302)
    noise_key = jax.random.fold_in(own_key, 1)
    noise = jnp.clip(jax.random.normal(noise_key, (NCAP, LCAP, D), jnp.float32), -4.0, 4.0)
    return planted_rows(own_key, key, noise, 0.125, 1.5, 3.5).astype(jnp.bfloat16)


def paired_weight(key, number):
    common = jax.random.normal(jax.random.fold_in(key, 9201), (D, D), jnp.float32)
    single = jax.random.normal(jax.random.fold_in(key, 9201 + number), (D, D), jnp.float32)
    mixed = 0.9 ** 0.5 * common + 0.1 ** 0.5 * single
    return jnp.clip(mixed * (D // 4) ** (-0.5), -1.0, 1.0)


def draw_query_weight(key, part):
    return paired_weight(key, 1).astype(jnp.bfloat16)


def draw_key_weight(key, part):
    return paired_weight(key, 2).astype(jnp.bfloat16)


def normal_values(rng, extent, scale, most, held_as=jnp.bfloat16):
    array = jax.random.normal(rng, extent, jnp.float32) * scale
    return jnp.minimum(jnp.maximum(array, -most), most).astype(held_as)


def setup_inputs(seed: int = 0) -> dict:
    key_of = jax.random.split(jax.random.key(seed), 16)
    pair_list = draw_pair_list(jax.random.fold_in(key_of[15], 71), 0)
    verify_order = draw_verify_order(jax.random.fold_in(key_of[15], 71), 0)
    image_slot = draw_image_slot(jax.random.fold_in(key_of[15], 71), 0)
    caption_slot = draw_caption_slot(jax.random.fold_in(key_of[15], 71), 0)
    images = draw_images(jax.random.fold_in(key_of[15], 71), 0)
    captions = draw_captions(jax.random.fold_in(key_of[15], 71), 0)
    query_weight = draw_query_weight(jax.random.fold_in(key_of[15], 71), 0)
    key_weight = draw_key_weight(jax.random.fold_in(key_of[15], 71), 0)
    value_weight = normal_values(key_of[8], (D, D), D ** -0.5, 0.21875)
    out_weight = normal_values(key_of[9], (D, D), (D // 4) ** -0.5, 0.4375)
    gain_attn = jnp.clip(1.0 + 0.1 * jax.random.normal(key_of[10], (D,), jnp.float32), 0.5, 1.5)
    in_weight = normal_values(key_of[11], (D, FF), D ** -0.5, 0.21875)
    back_weight = normal_values(key_of[12], (FF, D), FF ** -0.5, 0.109375)
    gain_ffn = jnp.clip(1.0 + 0.1 * jax.random.normal(key_of[13], (D,), jnp.float32), 0.5, 1.5)
    match_weight = normal_values(key_of[14], (D, 2), D ** -0.5, 0.21875)
    return {"pair_list": pair_list, "verify_order": verify_order, "image_slot": image_slot, "caption_slot": caption_slot, "images": images, "captions": captions, "query_weight": query_weight, "key_weight": key_weight, "value_weight": value_weight, "out_weight": out_weight, "gain_attn": gain_attn, "in_weight": in_weight, "back_weight": back_weight, "gain_ffn": gain_ffn, "match_weight": match_weight}


def norm_rows(hidden, gain):
    row_mean = lax.optimization_barrier(jnp.mean(hidden, axis=-1, keepdims=True))
    centred = hidden - row_mean
    row_var = lax.optimization_barrier(jnp.mean(centred * centred, axis=-1, keepdims=True))
    return centred * lax.rsqrt(row_var + 1e-06) * gain

def cross_layer(caption_rows, key_rows, value_rows, query_weight, out_weight, gain_attn, in_weight, back_weight, gain_ffn):
    pair_count, token_count, width = caption_rows.shape
    head_size = width // HEADS
    query = jnp.dot(caption_rows, query_weight, preferred_element_type=jnp.float32).astype(jnp.bfloat16)
    query = query.reshape(pair_count, token_count, HEADS, head_size)
    key_heads = key_rows.reshape(pair_count, -1, HEADS, head_size)
    value_heads = value_rows.reshape(pair_count, -1, HEADS, head_size)
    scores = jnp.einsum('pqhd,pkhd->phqk', query.astype(jnp.float32), key_heads.astype(jnp.float32)) / jnp.sqrt(jnp.float32(head_size))
    weights_attn = jax.nn.softmax(scores, axis=-1).astype(jnp.bfloat16)
    context = jnp.einsum('phqk,pkhd->pqhd', weights_attn.astype(jnp.float32), value_heads.astype(jnp.float32)).astype(jnp.bfloat16)
    context = context.reshape(pair_count, token_count, width)
    hidden = caption_rows.astype(jnp.float32) + jnp.dot(context, out_weight, preferred_element_type=jnp.float32)
    hidden = norm_rows(hidden, gain_attn).astype(jnp.bfloat16)
    inner = jax.nn.gelu(jnp.dot(hidden, in_weight, preferred_element_type=jnp.float32), approximate=False).astype(jnp.bfloat16)
    summed = hidden.astype(jnp.float32) + jnp.dot(inner, back_weight, preferred_element_type=jnp.float32)
    return norm_rows(summed, gain_ffn).astype(jnp.bfloat16)

def reference(pair_list, verify_order, image_slot, caption_slot, images, captions, query_weight, key_weight, value_weight, out_weight, gain_attn, in_weight, back_weight, gain_ffn, match_weight):

    def project_image(stored):
        return (jnp.dot(stored, key_weight, preferred_element_type=jnp.float32).astype(jnp.bfloat16), jnp.dot(stored, value_weight, preferred_element_type=jnp.float32).astype(jnp.bfloat16))
    keys_all, values_all = lax.map(project_image, images)
    pair_ids = jnp.take(pair_list, verify_order, axis=0)
    image_rows = jnp.take(image_slot, pair_ids[:, 0]).astype(jnp.int32).reshape(-1, PAIR_DEV)
    caption_rows_all = jnp.take(caption_slot, pair_ids[:, 1]).astype(jnp.int32).reshape(-1, PAIR_DEV)

    def score_group(rows):
        image_part, caption_part = rows
        caption_rows = jnp.take(captions, caption_part, axis=0)
        key_rows = jnp.take(keys_all, image_part, axis=0)
        value_rows = jnp.take(values_all, image_part, axis=0)
        return cross_layer(caption_rows, key_rows, value_rows, query_weight, out_weight, gain_attn, in_weight, back_weight, gain_ffn)
    merged = lax.map(score_group, (image_rows, caption_rows_all)).reshape(PAIRS, LCAP, D)
    match_logits = jnp.dot(merged[:, 0, :], match_weight, preferred_element_type=jnp.float32)
    return (merged, match_logits)
```

```python
import functools

import jax
import jax.numpy as jnp
from jax import lax
from jax.experimental import pallas as pl
from jax.experimental.pallas import tpu as pltpu
from jax.sharding import PartitionSpec as P

HEADS = 12
IMG_MOST = 2
CORES = 2
PACK = 65536
KEY_PAD = 256
LANES = 128
GROUP = 256
F32 = jnp.float32
BF16 = jnp.bfloat16

SMEM = pl.BlockSpec(memory_space=pltpu.SMEM)
VMEM = pl.BlockSpec(memory_space=pltpu.VMEM)


def params(mib):
    return pltpu.CompilerParams(vmem_limit_bytes=mib * 1024 * 1024)


def norm_rows(hidden, gain):
    row_mean = jnp.mean(hidden, axis=-1, keepdims=True)
    centred = hidden - row_mean
    row_var = jnp.mean(centred * centred, axis=-1, keepdims=True)
    return centred * lax.rsqrt(row_var + 1e-06) * gain


def table_kernel(image_local, caption_count, pairs, order, image_slot, caption_slot, table, place, count):
    img_count = count.shape[0]
    me = lax.axis_index("img")
    for owner in range(img_count):
        count[owner] = 0
        for rank in range(IMG_MOST):
            for column in range(caption_count):
                table[owner * caption_count + column, rank] = 0
    for row in range(order.shape[0]):
        pair = order[row]
        image = image_slot[pairs[0, pair]]
        caption = caption_slot[pairs[1, pair]]
        owner = image // image_local
        rank = count[owner]
        count[owner] = rank + 1
        entry = (image - owner * image_local) * PACK + caption
        for column in range(caption_count):
            table[owner * caption_count + column, rank] = entry
        place[row] = jnp.bitwise_xor(owner, me) * IMG_MOST + rank


def make_table(pairs, order, image_slot, caption_slot, image_local, img_count, caption_count):
    return pl.pallas_call(
        functools.partial(table_kernel, image_local, caption_count),
        out_shape=(
            jax.ShapeDtypeStruct((img_count * caption_count, LANES), jnp.int32),
            jax.ShapeDtypeStruct(order.shape, jnp.int32),
        ),
        in_specs=[SMEM] * 4,
        out_specs=(SMEM, SMEM),
        scratch_shapes=[pltpu.SMEM((img_count,), jnp.int32)],
        name="slot_table",
    )(pairs, order, image_slot, caption_slot)


def read_slot(table, cap_count, column, distance, rank, caption_local):
    verifier = jnp.bitwise_xor(lax.axis_index("img"), distance)
    entry = table[verifier * cap_count + column, rank]
    caption = jnp.bitwise_and(entry, PACK - 1)
    owner = caption // caption_local
    return lax.shift_right_logical(entry, 16), owner, caption - owner * caption_local


def pick_kernel(step, cap_count, chunks, table, own, sibling, *outs):
    mine = lax.axis_index("cap")
    asker = jnp.bitwise_xor(mine, step * CORES)
    for chunk, out in zip(chunks, outs):
        for index, distance in enumerate(chunk):
            for rank in range(IMG_MOST):
                _, owner, local = read_slot(table, cap_count, asker, distance, rank, own.shape[0])
                near = owner == jnp.bitwise_xor(mine, 1)

                @pl.when(near)
                def _():
                    out[index * IMG_MOST + rank] = sibling[local]

                @pl.when(jnp.logical_not(near))
                def _():
                    out[index * IMG_MOST + rank] = own[local]


def pick_blocks(step, cap_count, chunks, table, own, sibling):
    outs = tuple(
        jax.ShapeDtypeStruct((len(chunk) * IMG_MOST,) + own.shape[1:], own.dtype) for chunk in chunks
    )
    return pl.pallas_call(
        functools.partial(pick_kernel, step, cap_count, chunks),
        out_shape=outs,
        in_specs=[SMEM, VMEM, VMEM],
        out_specs=(VMEM,) * len(outs),
        compiler_params=params(8),
        cost_estimate=pl.CostEstimate(flops=0, bytes_accessed=1 << 20, transcendentals=0),
        name="pick_captions",
    )(table, own, sibling)


def project_kernel(images, key_weight, value_weight, keys, values):
    rows = images.shape[1]
    patches = images[0]
    for weight, out in ((key_weight, keys), (value_weight, values)):
        out[0, rows // 16 * 16 :, :] = jnp.zeros((KEY_PAD - rows // 16 * 16, out.shape[2]), BF16)
        out[0, :rows, :] = jnp.dot(patches, weight[...], preferred_element_type=F32).astype(BF16)


def project_images(images, key_weight, value_weight):
    count, rows, width = images.shape
    whole = pl.BlockSpec((width, width), lambda i: (0, 0))
    out = jax.ShapeDtypeStruct((count, KEY_PAD, width), BF16)
    return pl.pallas_call(
        project_kernel,
        out_shape=(out, out),
        grid=(count,),
        in_specs=[pl.BlockSpec((1, rows, width), lambda i: (i, 0, 0)), whole, whole],
        out_specs=(pl.BlockSpec((1, KEY_PAD, width), lambda i: (i, 0, 0)),) * 2,
        compiler_params=params(16),
        cost_estimate=pl.CostEstimate(
            flops=4 * count * KEY_PAD * width * width,
            bytes_accessed=2 * (2 * width * width + count * (rows + 2 * KEY_PAD) * width),
            transcendentals=0,
        ),
        name="project_images",
    )(images, key_weight, value_weight)


def attend_kernel(key_rows, cap_count, far_count, chunk, table, own, sibling, *rest):
    far = rest[:far_count]
    keys, values, query_weight, out_weight, gain = rest[far_count : far_count + 5]
    outs = rest[far_count + 5 : far_count + 5 + len(chunk)]
    rows, query, context = rest[far_count + 5 + len(chunk) :]
    column = lax.axis_index("cap")
    tokens, width = own.shape[1], own.shape[2]
    head_size = width // HEADS
    heads = GROUP // head_size
    pair_count = len(chunk) * IMG_MOST
    images = []
    for pair in range(pair_count):
        image, owner, local = read_slot(
            table, cap_count, column, chunk[pair // IMG_MOST], pair % IMG_MOST, own.shape[0]
        )
        images.append(image)
        apart = jnp.bitwise_xor(owner, column)

        @pl.when(apart == 0)
        def _():
            rows[pair] = own[local]

        @pl.when(apart == 1)
        def _():
            rows[pair] = sibling[local]

        for step in range(far_count):

            @pl.when(apart // CORES == step + 1)
            def _():
                rows[pair] = far[step][pair]

    flat = rows[...].reshape(pair_count * tokens, width)
    query[...] = jnp.dot(flat, query_weight[...], preferred_element_type=F32).astype(BF16)
    lane_head = lax.broadcasted_iota(jnp.int32, (tokens, GROUP), 1) // head_size
    visible = lax.broadcasted_iota(jnp.int32, (heads * tokens, KEY_PAD), 1) < key_rows
    scale = 1.0 / float(head_size) ** 0.5
    spans = [slice(group * GROUP, (group + 1) * GROUP) for group in range(width // GROUP)]

    def score(pair):
        found = []
        for span in spans:
            part = query[pair * tokens : (pair + 1) * tokens, span]
            stacked = jnp.concatenate(
                [jnp.where(lane_head == head, part, jnp.zeros_like(part)) for head in range(heads)],
                axis=0,
            )
            found.append(
                lax.dot_general(
                    stacked,
                    keys[images[pair], :, span],
                    (((1,), (1,)), ((), ())),
                    preferred_element_type=F32,
                )
            )
        return found

    def mix(pair, found):
        for span, scores in zip(spans, found):
            scores = jnp.where(visible, scores * scale, -jnp.inf)
            top = jnp.max(scores, axis=-1, keepdims=True)
            weights = jnp.exp(scores - top)
            share = 1.0 / jnp.sum(weights, axis=-1, keepdims=True)
            probs = (weights * share).astype(BF16)
            mixed = jnp.dot(probs, values[images[pair], :, span], preferred_element_type=F32)
            joined = mixed[:tokens]
            for head in range(1, heads):
                joined = jnp.where(lane_head == head, mixed[head * tokens : (head + 1) * tokens], joined)
            context[pair * tokens : (pair + 1) * tokens, span] = joined.astype(BF16)

    found = score(0)
    for pair in range(pair_count):
        later = score(pair + 1) if pair + 1 < pair_count else None
        mix(pair, found)
        found = later
    hidden = flat.astype(F32) + jnp.dot(context[...], out_weight[...], preferred_element_type=F32)
    hidden = norm_rows(hidden, gain[...]).astype(BF16).reshape(pair_count, tokens, width)
    for index, out in enumerate(outs):
        out[...] = hidden[index * IMG_MOST : (index + 1) * IMG_MOST]


def attend(key_rows, cap_count, chunk, table, own, sibling, far, keys, values, query_weight, out_weight, gain):
    tokens, width = own.shape[1:]
    pair_count = len(chunk) * IMG_MOST
    rows = pair_count * tokens
    return pl.pallas_call(
        functools.partial(attend_kernel, key_rows, cap_count, len(far), chunk),
        out_shape=(jax.ShapeDtypeStruct((IMG_MOST, tokens, width), BF16),) * len(chunk),
        in_specs=[SMEM] + [VMEM] * (7 + len(far)),
        out_specs=(VMEM,) * len(chunk),
        scratch_shapes=[
            pltpu.VMEM((pair_count, tokens, width), BF16),
            pltpu.VMEM((rows, width), BF16),
            pltpu.VMEM((rows, width), BF16),
        ],
        compiler_params=params(16),
        cost_estimate=pl.CostEstimate(
            flops=4 * rows * width * width + 4 * rows * GROUP * KEY_PAD * HEADS,
            bytes_accessed=8 * width * width,
            transcendentals=rows * HEADS * KEY_PAD,
        ),
        name="attend",
    )(table, own, sibling, *far, keys, values, query_weight, out_weight, gain)


TILES = 3


def feed_rows(parts, gain, in_weight, back_weight):
    count, tokens, width = parts[0].shape
    step = in_weight.shape[1] // TILES
    flat = jnp.concatenate([part[...] for part in parts], axis=0).reshape(-1, width)
    total = flat.astype(F32)
    for tile in range(TILES):
        span = slice(tile * step, (tile + 1) * step)
        inner = jnp.dot(flat, in_weight[:, span], preferred_element_type=F32)
        inner = (0.5 * inner * (1.0 + lax.erf(inner * (0.5**0.5)))).astype(BF16)
        total = total + jnp.dot(inner, back_weight[span, :], preferred_element_type=F32)
    return norm_rows(total, gain[...]).astype(BF16).reshape(-1, tokens, width)


def feed_first_kernel(gain, in_weight, back_weight, *rest):
    parts, out = rest[:-1], rest[-1]
    out[...] = feed_rows(parts, gain, in_weight, back_weight)


def feed_last_kernel(first_parts, last_parts, place, gain, match_weight, in_weight, back_weight, earlier, *rest):
    parts = rest[: len(last_parts)]
    merged, logits, done, first = rest[len(last_parts) :]
    slots = len(first_parts) * IMG_MOST
    done[:slots] = earlier[...]
    done[slots:] = feed_rows(parts, gain, in_weight, back_weight)
    for row in range(merged.shape[0]):
        slot = place[row]
        distance = slot // IMG_MOST
        spot = jnp.int32(0)
        for index, listed in enumerate(first_parts + last_parts):
            spot = jnp.where(distance == listed, index, spot)
        block = done[spot * IMG_MOST + slot % IMG_MOST]
        merged[row] = block
        first[row : row + 1, :] = block[0:1, :].astype(F32)
    logits[...] = lax.dot_general(
        match_weight[...], first[...].astype(BF16), (((1,), (1,)), ((), ())), preferred_element_type=F32
    )


def feed_cost(rows, width, inner_width):
    return pl.CostEstimate(
        flops=4 * rows * width * inner_width,
        bytes_accessed=4 * width * inner_width,
        transcendentals=rows * inner_width,
    )


def feed_first(parts, gain, in_weight, back_weight):
    count, tokens, width = parts[0].shape
    slots = len(parts) * count
    return pl.pallas_call(
        feed_first_kernel,
        out_shape=jax.ShapeDtypeStruct((slots, tokens, width), BF16),
        in_specs=[VMEM] * (3 + len(parts)),
        out_specs=VMEM,
        compiler_params=params(16),
        cost_estimate=feed_cost(slots * tokens, width, in_weight.shape[1]),
        name="feed_first",
    )(gain, in_weight, back_weight, *parts)


def feed_last(first_parts, last_parts, place, gain, match_weight, in_weight, back_weight, earlier, parts):
    count, tokens, width = parts[0].shape
    rows = place.shape[0]
    slots = (len(first_parts) + len(last_parts)) * count
    return pl.pallas_call(
        functools.partial(feed_last_kernel, first_parts, last_parts),
        out_shape=(
            jax.ShapeDtypeStruct((rows, tokens, width), BF16),
            jax.ShapeDtypeStruct((match_weight.shape[0], rows), F32),
        ),
        in_specs=[SMEM] + [VMEM] * (5 + len(parts)),
        out_specs=(VMEM, VMEM),
        scratch_shapes=[pltpu.VMEM((slots, tokens, width), BF16), pltpu.VMEM((rows, width), F32)],
        compiler_params=params(16),
        cost_estimate=feed_cost(len(parts) * count * tokens, width, in_weight.shape[1]),
        name="feed_last",
    )(place, gain, match_weight, in_weight, back_weight, earlier, *parts)


def body(
    pair_list,
    verify_order,
    image_slot,
    caption_slot,
    images,
    captions,
    query_weight,
    key_weight,
    value_weight,
    out_weight,
    gain_attn,
    in_weight,
    back_weight,
    gain_ffn,
    match_weight,
):
    img_count = lax.axis_size("img")
    cap_count = lax.axis_size("cap")
    far_steps = range(1, cap_count // CORES)
    half, quarter = img_count // 2, img_count // 4
    chunks = (tuple(range(img_count - 1, half - 1, -1)), tuple(range(half - 1, -1, -1)))
    first_parts = chunks[0][:quarter] + chunks[1][half - quarter :]
    last_parts = chunks[0][quarter:] + chunks[1][: half - quarter]

    def swap(array, axis, distance):
        size = lax.axis_size(axis)
        return lax.ppermute(array, axis, [(peer, peer ^ distance) for peer in range(size)])

    sibling = swap(captions, "cap", 1)
    table, place = make_table(
        pair_list.T, verify_order, image_slot, caption_slot, images.shape[0], img_count, cap_count
    )
    table = lax.all_to_all(table, ("img", "cap"), split_axis=0, concat_axis=0, tiled=True)
    keys, values = project_images(images, key_weight, value_weight)
    far = [[] for _ in chunks]
    for step in far_steps:
        picked = pick_blocks(step, cap_count, chunks, table, captions, sibling)
        for blocks, block in zip(far, picked):
            blocks.append(swap(block, "cap", step * CORES))
    gain_attn = gain_attn.reshape(1, -1)
    gain_ffn = gain_ffn.reshape(1, -1)
    hidden = {}
    for index, chunk in enumerate(chunks):
        blocks = attend(
            images.shape[1],
            cap_count,
            chunk,
            table,
            captions,
            sibling,
            far[index],
            keys,
            values,
            query_weight,
            out_weight,
            gain_attn,
        )
        if index == 0:
            blocks, far = lax.optimization_barrier((blocks, far))
        for distance, block in zip(chunk, blocks):
            hidden[distance] = swap(block, "img", distance) if distance else block
    earlier = feed_first([hidden[part] for part in first_parts], gain_ffn, in_weight, back_weight)
    merged, logits = feed_last(
        first_parts,
        last_parts,
        place,
        gain_ffn,
        match_weight.T,
        in_weight,
        back_weight,
        earlier,
        [hidden[part] for part in last_parts],
    )
    return merged, logits.T


def solution(mesh):
    placed = (
        P(),
        P(("img", "cap")),
        P(),
        P(),
        P("img", None, None),
        P("cap", None, None),
        P(),
        P(),
        P(),
        P(),
        P(),
        P(),
        P(),
        P(),
        P(),
    )
    return jax.shard_map(
        body,
        mesh=mesh,
        in_specs=placed,
        out_specs=(P(("img", "cap"), None, None), P(("img", "cap"), None)),
        check_vma=False,
    )
```

```python
import functools

import jax
import jax.numpy as jnp
from jax import lax
from jax.experimental import pallas as pl
from jax.experimental.pallas import tpu as pltpu
from jax.sharding import PartitionSpec as P

HEADS = 12
IMG_MOST = 2
CORES = 2
PACK = 65536
KEY_PAD = 256
LANES = 128
GROUP = 256
F32 = jnp.float32
BF16 = jnp.bfloat16
SMALL = pl.CostEstimate(flops=1 << 16, bytes_accessed=1 << 10, transcendentals=0)

SMEM = pl.BlockSpec(memory_space=pltpu.SMEM)
VMEM = pl.BlockSpec(memory_space=pltpu.VMEM)


def params(mib):
    return pltpu.CompilerParams(vmem_limit_bytes=mib * 1024 * 1024)


def norm_rows(hidden, gain):
    row_mean = jnp.mean(hidden, axis=-1, keepdims=True)
    centred = hidden - row_mean
    row_var = jnp.mean(centred * centred, axis=-1, keepdims=True)
    return centred * lax.rsqrt(row_var + 1e-06) * gain


def table_kernel(image_local, caption_count, pairs, order, image_slot, caption_slot, table, place, count):
    img_count = count.shape[0]
    me = lax.axis_index("img")
    for owner in range(img_count):
        count[owner] = 0
        for rank in range(IMG_MOST):
            for column in range(caption_count):
                table[owner * caption_count + column, rank] = 0
    for row in range(order.shape[0]):
        pair = order[row]
        image = image_slot[pairs[0, pair]]
        caption = caption_slot[pairs[1, pair]]
        owner = image // image_local
        rank = count[owner]
        count[owner] = rank + 1
        entry = (image - owner * image_local) * PACK + caption
        for column in range(caption_count):
            table[owner * caption_count + column, rank] = entry
        place[row] = jnp.bitwise_xor(owner, me) * IMG_MOST + rank


def make_table(pairs, order, image_slot, caption_slot, image_local, img_count, caption_count):
    return pl.pallas_call(
        functools.partial(table_kernel, image_local, caption_count),
        out_shape=(
            jax.ShapeDtypeStruct((img_count * caption_count, LANES), jnp.int32),
            jax.ShapeDtypeStruct(order.shape, jnp.int32),
        ),
        in_specs=[SMEM] * 4,
        out_specs=(SMEM, SMEM),
        scratch_shapes=[pltpu.SMEM((img_count,), jnp.int32)],
        name="slot_table",
    )(pairs, order, image_slot, caption_slot)


def read_slot(table, cap_count, column, distance, rank, caption_local):
    verifier = jnp.bitwise_xor(lax.axis_index("img"), distance)
    entry = table[verifier * cap_count + column, rank]
    caption = jnp.bitwise_and(entry, PACK - 1)
    owner = caption // caption_local
    return lax.shift_right_logical(entry, 16), owner, caption - owner * caption_local


def pick_kernel(step, cap_count, chunks, table, own, sibling, *outs):
    mine = lax.axis_index("cap")
    asker = jnp.bitwise_xor(mine, step * CORES)
    for chunk, out in zip(chunks, outs):
        for index, distance in enumerate(chunk):
            for rank in range(IMG_MOST):
                _, owner, local = read_slot(table, cap_count, asker, distance, rank, own.shape[0])
                near = owner == jnp.bitwise_xor(mine, 1)

                @pl.when(near)
                def _():
                    out[index * IMG_MOST + rank] = sibling[local]

                @pl.when(jnp.logical_not(near))
                def _():
                    out[index * IMG_MOST + rank] = own[local]


def pick_blocks(step, cap_count, chunks, table, own, sibling):
    outs = tuple(
        jax.ShapeDtypeStruct((len(chunk) * IMG_MOST,) + own.shape[1:], own.dtype) for chunk in chunks
    )
    return pl.pallas_call(
        functools.partial(pick_kernel, step, cap_count, chunks),
        out_shape=outs,
        in_specs=[SMEM, VMEM, VMEM],
        out_specs=(VMEM,) * len(outs),
        compiler_params=params(8),
        cost_estimate=pl.CostEstimate(flops=0, bytes_accessed=1 << 20, transcendentals=0),
        name="pick_captions",
    )(table, own, sibling)


def project_kernel(images, key_weight, value_weight, keys, values):
    rows = images.shape[1]
    patches = images[0]
    for weight, out in ((key_weight, keys), (value_weight, values)):
        out[0, rows // 16 * 16 :, :] = jnp.zeros((KEY_PAD - rows // 16 * 16, out.shape[2]), BF16)
        out[0, :rows, :] = jnp.dot(patches, weight[...], preferred_element_type=F32).astype(BF16)


def project_images(images, key_weight, value_weight):
    count, rows, width = images.shape
    whole = pl.BlockSpec((width, width), lambda i: (0, 0))
    out = jax.ShapeDtypeStruct((count, KEY_PAD, width), BF16)
    return pl.pallas_call(
        project_kernel,
        out_shape=(out, out),
        grid=(count,),
        in_specs=[pl.BlockSpec((1, rows, width), lambda i: (i, 0, 0)), whole, whole],
        out_specs=(pl.BlockSpec((1, KEY_PAD, width), lambda i: (i, 0, 0)),) * 2,
        compiler_params=params(16),
        cost_estimate=SMALL,
        name="project_images",
    )(images, key_weight, value_weight)


def attend_kernel(key_rows, cap_count, far_count, chunk, table, own, sibling, *rest):
    far = rest[:far_count]
    keys, values, query_weight, out_weight, gain = rest[far_count : far_count + 5]
    outs = rest[far_count + 5 : far_count + 5 + len(chunk)]
    rows, query, context = rest[far_count + 5 + len(chunk) :]
    column = lax.axis_index("cap")
    tokens, width = own.shape[1], own.shape[2]
    head_size = width // HEADS
    heads = GROUP // head_size
    pair_count = len(chunk) * IMG_MOST
    images = []
    for pair in range(pair_count):
        image, owner, local = read_slot(
            table, cap_count, column, chunk[pair // IMG_MOST], pair % IMG_MOST, own.shape[0]
        )
        images.append(image)
        apart = jnp.bitwise_xor(owner, column)

        @pl.when(apart == 0)
        def _():
            rows[pair] = own[local]

        @pl.when(apart == 1)
        def _():
            rows[pair] = sibling[local]

        for step in range(far_count):

            @pl.when(apart // CORES == step + 1)
            def _():
                rows[pair] = far[step][pair]

    flat = rows[...].reshape(pair_count * tokens, width)
    query[...] = jnp.dot(flat, query_weight[...], preferred_element_type=F32).astype(BF16)
    lane_head = lax.broadcasted_iota(jnp.int32, (tokens, GROUP), 1) // head_size
    visible = lax.broadcasted_iota(jnp.int32, (heads * tokens, KEY_PAD), 1) < key_rows
    scale = 1.0 / float(head_size) ** 0.5
    spans = [slice(group * GROUP, (group + 1) * GROUP) for group in range(width // GROUP)]

    def score(pair):
        found = []
        for span in spans:
            part = query[pair * tokens : (pair + 1) * tokens, span]
            stacked = jnp.concatenate(
                [jnp.where(lane_head == head, part, jnp.zeros_like(part)) for head in range(heads)],
                axis=0,
            )
            found.append(
                lax.dot_general(
                    stacked,
                    keys[images[pair], :, span],
                    (((1,), (1,)), ((), ())),
                    preferred_element_type=F32,
                )
            )
        return found

    def mix(pair, found):
        for span, scores in zip(spans, found):
            scores = jnp.where(visible, scores * scale, -jnp.inf)
            top = jnp.max(scores, axis=-1, keepdims=True)
            weights = jnp.exp(scores - top)
            share = 1.0 / jnp.sum(weights, axis=-1, keepdims=True)
            probs = (weights * share).astype(BF16)
            mixed = jnp.dot(probs, values[images[pair], :, span], preferred_element_type=F32)
            joined = mixed[:tokens]
            for head in range(1, heads):
                joined = jnp.where(lane_head == head, mixed[head * tokens : (head + 1) * tokens], joined)
            context[pair * tokens : (pair + 1) * tokens, span] = joined.astype(BF16)

    found = score(0)
    for pair in range(pair_count):
        later = score(pair + 1) if pair + 1 < pair_count else None
        mix(pair, found)
        found = later
    hidden = flat.astype(F32) + jnp.dot(context[...], out_weight[...], preferred_element_type=F32)
    hidden = norm_rows(hidden, gain[...]).astype(BF16).reshape(pair_count, tokens, width)
    for index, out in enumerate(outs):
        out[...] = hidden[index * IMG_MOST : (index + 1) * IMG_MOST]


def attend(key_rows, cap_count, chunk, table, own, sibling, far, keys, values, query_weight, out_weight, gain):
    tokens, width = own.shape[1:]
    pair_count = len(chunk) * IMG_MOST
    rows = pair_count * tokens
    return pl.pallas_call(
        functools.partial(attend_kernel, key_rows, cap_count, len(far), chunk),
        out_shape=(jax.ShapeDtypeStruct((IMG_MOST, tokens, width), BF16),) * len(chunk),
        in_specs=[SMEM] + [VMEM] * (7 + len(far)),
        out_specs=(VMEM,) * len(chunk),
        scratch_shapes=[
            pltpu.VMEM((pair_count, tokens, width), BF16),
            pltpu.VMEM((rows, width), BF16),
            pltpu.VMEM((rows, width), BF16),
        ],
        compiler_params=params(16),
        cost_estimate=SMALL,
        name="attend",
    )(table, own, sibling, *far, keys, values, query_weight, out_weight, gain)


TILES = 3


def feed_rows(parts, gain, in_weight, back_weight):
    count, tokens, width = parts[0].shape
    step = in_weight.shape[1] // TILES
    flat = jnp.concatenate([part[...] for part in parts], axis=0).reshape(-1, width)
    total = flat.astype(F32)
    for tile in range(TILES):
        span = slice(tile * step, (tile + 1) * step)
        inner = jnp.dot(flat, in_weight[:, span], preferred_element_type=F32)
        inner = (0.5 * inner * (1.0 + lax.erf(inner * (0.5**0.5)))).astype(BF16)
        total = total + jnp.dot(inner, back_weight[span, :], preferred_element_type=F32)
    return norm_rows(total, gain[...]).astype(BF16).reshape(-1, tokens, width)


def feed_first_kernel(gain, in_weight, back_weight, *rest):
    parts, out = rest[:-1], rest[-1]
    out[...] = feed_rows(parts, gain, in_weight, back_weight)


def feed_last_kernel(first_parts, last_parts, place, gain, match_weight, in_weight, back_weight, earlier, *rest):
    parts = rest[: len(last_parts)]
    merged, logits, done, first = rest[len(last_parts) :]
    slots = len(first_parts) * IMG_MOST
    done[:slots] = earlier[...]
    done[slots:] = feed_rows(parts, gain, in_weight, back_weight)
    for row in range(merged.shape[0]):
        slot = place[row]
        distance = slot // IMG_MOST
        spot = jnp.int32(0)
        for index, listed in enumerate(first_parts + last_parts):
            spot = jnp.where(distance == listed, index, spot)
        block = done[spot * IMG_MOST + slot % IMG_MOST]
        merged[row] = block
        first[row : row + 1, :] = block[0:1, :].astype(F32)
    logits[...] = lax.dot_general(
        match_weight[...], first[...].astype(BF16), (((1,), (1,)), ((), ())), preferred_element_type=F32
    )


def feed_cost(rows, width, inner_width):
    return pl.CostEstimate(
        flops=4 * rows * width * inner_width,
        bytes_accessed=4 * width * inner_width,
        transcendentals=rows * inner_width,
    )


def feed_first(parts, gain, in_weight, back_weight):
    count, tokens, width = parts[0].shape
    slots = len(parts) * count
    return pl.pallas_call(
        feed_first_kernel,
        out_shape=jax.ShapeDtypeStruct((slots, tokens, width), BF16),
        in_specs=[VMEM] * (3 + len(parts)),
        out_specs=VMEM,
        compiler_params=params(16),
        cost_estimate=feed_cost(slots * tokens, width, in_weight.shape[1]),
        name="feed_first",
    )(gain, in_weight, back_weight, *parts)


def feed_last(first_parts, last_parts, place, gain, match_weight, in_weight, back_weight, earlier, parts):
    count, tokens, width = parts[0].shape
    rows = place.shape[0]
    slots = (len(first_parts) + len(last_parts)) * count
    return pl.pallas_call(
        functools.partial(feed_last_kernel, first_parts, last_parts),
        out_shape=(
            jax.ShapeDtypeStruct((rows, tokens, width), BF16),
            jax.ShapeDtypeStruct((match_weight.shape[0], rows), F32),
        ),
        in_specs=[SMEM] + [VMEM] * (5 + len(parts)),
        out_specs=(VMEM, VMEM),
        scratch_shapes=[pltpu.VMEM((slots, tokens, width), BF16), pltpu.VMEM((rows, width), F32)],
        compiler_params=params(16),
        cost_estimate=feed_cost(len(parts) * count * tokens, width, in_weight.shape[1]),
        name="feed_last",
    )(place, gain, match_weight, in_weight, back_weight, earlier, *parts)


def body(
    pair_list,
    verify_order,
    image_slot,
    caption_slot,
    images,
    captions,
    query_weight,
    key_weight,
    value_weight,
    out_weight,
    gain_attn,
    in_weight,
    back_weight,
    gain_ffn,
    match_weight,
):
    img_count = lax.axis_size("img")
    cap_count = lax.axis_size("cap")
    far_steps = range(1, cap_count // CORES)
    half, quarter = img_count // 2, img_count // 4
    distances = tuple(range(img_count - 1, -1, -1))
    first_parts, last_parts = distances[:half], distances[half:]
    chunks = (distances[:quarter], distances[quarter:half], distances[half:])

    def swap(array, axis, distance):
        size = lax.axis_size(axis)
        return lax.ppermute(array, axis, [(peer, peer ^ distance) for peer in range(size)])

    sibling = swap(captions, "cap", 1)
    table, place = make_table(
        pair_list.T, verify_order, image_slot, caption_slot, images.shape[0], img_count, cap_count
    )
    table = lax.all_to_all(table, ("img", "cap"), split_axis=0, concat_axis=0, tiled=True)
    keys, values = project_images(images, key_weight, value_weight)
    far = [[] for _ in chunks]
    for step in far_steps:
        picked = pick_blocks(step, cap_count, chunks, table, captions, sibling)
        for blocks, block in zip(far, picked):
            blocks.append(swap(block, "cap", step * CORES))
    gain_attn = gain_attn.reshape(1, -1)
    gain_ffn = gain_ffn.reshape(1, -1)
    hidden = {}
    for index, chunk in enumerate(chunks):
        if index == 2:
            sent = [hidden[distance] for distance in chunks[0]]
            table, sent = lax.optimization_barrier((table, sent))
            hidden.update(zip(chunks[0], sent))
        blocks = attend(
            images.shape[1],
            cap_count,
            chunk,
            table,
            captions,
            sibling,
            far[index],
            keys,
            values,
            query_weight,
            out_weight,
            gain_attn,
        )
        for distance, block in zip(chunk, blocks):
            hidden[distance] = swap(block, "img", distance) if distance else block
    earlier = feed_first([hidden[part] for part in first_parts], gain_ffn, in_weight, back_weight)
    merged, logits = feed_last(
        first_parts,
        last_parts,
        place,
        gain_ffn,
        match_weight.T,
        in_weight,
        back_weight,
        earlier,
        [hidden[part] for part in last_parts],
    )
    return merged, logits.T


def solution(mesh):
    placed = (
        P(),
        P(("img", "cap")),
        P(),
        P(),
        P("img", None, None),
        P("cap", None, None),
        P(),
        P(),
        P(),
        P(),
        P(),
        P(),
        P(),
        P(),
        P(),
    )
    return jax.shard_map(
        body,
        mesh=mesh,
        in_specs=placed,
        out_specs=(P(("img", "cap"), None, None), P(("img", "cap"), None)),
        check_vma=False,
    )
```

```python
import functools

import jax
import jax.numpy as jnp
from jax import lax
from jax.experimental import pallas as pl
from jax.experimental.pallas import tpu as pltpu
from jax.sharding import PartitionSpec as P

HEADS = 12
IMG_MOST = 2
PIECES = 4
CORES = 2
PACK = 65536
KEY_PAD = 256
LANES = 128
GROUP = 256
F32 = jnp.float32
BF16 = jnp.bfloat16
SMALL = pl.CostEstimate(flops=1 << 16, bytes_accessed=1 << 10, transcendentals=0)

SMEM = pl.BlockSpec(memory_space=pltpu.SMEM)
VMEM = pl.BlockSpec(memory_space=pltpu.VMEM)
ANY = pl.BlockSpec(memory_space=pl.ANY)


def params(mib):
    return pltpu.CompilerParams(vmem_limit_bytes=mib * 1024 * 1024)


def norm_rows(hidden, gain):
    row_mean = jnp.mean(hidden, axis=-1, keepdims=True)
    centred = hidden - row_mean
    row_var = jnp.mean(centred * centred, axis=-1, keepdims=True)
    return centred * lax.rsqrt(row_var + 1e-06) * gain


def table_kernel(image_local, caption_count, pairs, order, image_slot, caption_slot, table, place, count):
    img_count = count.shape[0]
    me = lax.axis_index("img")
    for owner in range(img_count):
        count[owner] = 0
        for rank in range(IMG_MOST if img_count * IMG_MOST > order.shape[0] else 0):
            for column in range(caption_count):
                table[owner * caption_count + column, rank] = 0
    for row in range(order.shape[0]):
        pair = order[row]
        image = image_slot[pairs[0, pair]]
        caption = caption_slot[pairs[1, pair]]
        owner = image // image_local
        rank = count[owner]
        count[owner] = rank + 1
        entry = (image - owner * image_local) * PACK + caption
        for column in range(caption_count):
            table[owner * caption_count + column, rank] = entry
        place[row] = jnp.bitwise_xor(owner, me) * IMG_MOST + rank


def make_table(pairs, order, image_slot, caption_slot, image_local, img_count, caption_count):
    return pl.pallas_call(
        functools.partial(table_kernel, image_local, caption_count),
        out_shape=(
            jax.ShapeDtypeStruct((img_count * caption_count, LANES), jnp.int32),
            jax.ShapeDtypeStruct(order.shape, jnp.int32),
        ),
        in_specs=[SMEM] * 4,
        out_specs=(SMEM, SMEM),
        scratch_shapes=[pltpu.SMEM((img_count,), jnp.int32)],
        name="slot_table",
    )(pairs, order, image_slot, caption_slot)


def split_entry(entry, caption_local):
    caption = jnp.bitwise_and(entry, PACK - 1)
    owner = caption // caption_local
    return lax.shift_right_logical(entry, 16), owner, caption - owner * caption_local


def pick_kernel(step, cap_count, chunks, table, captions, sibling, slots, *rest):
    outs, own, sems = rest[: len(chunks)], rest[len(chunks)], rest[len(chunks) + 1]
    piece = own.shape[0] // PIECES
    copies = []
    for index in range(PIECES):
        span = pl.ds(index * piece, piece)
        copies.append(pltpu.make_async_copy(captions.at[span], own.at[span], sems.at[index]))
        copies[-1].start()
    me = lax.axis_index("img")
    mine = lax.axis_index("cap")
    asker = jnp.bitwise_xor(mine, step * CORES)
    picks = []
    for chunk, out in zip(chunks, outs):
        for index, distance in enumerate(chunk):
            verifier = jnp.bitwise_xor(me, distance) * cap_count
            for rank in range(IMG_MOST):
                slots[distance * IMG_MOST + rank] = table[verifier + mine, rank]
                _, owner, local = split_entry(table[verifier + asker, rank], own.shape[0])
                near = owner == jnp.bitwise_xor(mine, 1)
                picks.append((out, index * IMG_MOST + rank, near, local))

                @pl.when(near)
                def _():
                    out[index * IMG_MOST + rank] = sibling[local]

    for copy in copies:
        copy.wait()
    for out, spot, near, local in picks:

        @pl.when(jnp.logical_not(near))
        def _():
            out[spot] = own[local]


def pick_blocks(step, cap_count, chunks, table, own, sibling):
    slot_count = sum(len(chunk) for chunk in chunks) * IMG_MOST
    outs = tuple(
        jax.ShapeDtypeStruct((len(chunk) * IMG_MOST,) + own.shape[1:], own.dtype) for chunk in chunks
    )
    return pl.pallas_call(
        functools.partial(pick_kernel, step, cap_count, chunks),
        out_shape=(jax.ShapeDtypeStruct((slot_count,), jnp.int32),) + outs,
        in_specs=[SMEM, ANY, VMEM],
        out_specs=(SMEM,) + (VMEM,) * len(outs),
        scratch_shapes=[pltpu.VMEM(own.shape, own.dtype), pltpu.SemaphoreType.DMA((PIECES,))],
        compiler_params=params(8),
        cost_estimate=SMALL,
        name="pick_captions",
    )(table, own, sibling)


def project_kernel(images, key_weight, value_weight, keys, values):
    count, rows, width = images.shape
    whole = rows // 16 * 16
    for image in range(count):
        for weight, out in ((key_weight, keys), (value_weight, values)):
            out[image, whole:, :] = jnp.zeros((KEY_PAD - whole, width), BF16)
            out[image, :rows, :] = jnp.dot(images[image], weight[...], preferred_element_type=F32).astype(BF16)


def project_images(images, key_weight, value_weight):
    count, rows, width = images.shape
    out = jax.ShapeDtypeStruct((count, KEY_PAD, width), BF16)
    return pl.pallas_call(
        project_kernel,
        out_shape=(out, out),
        in_specs=[VMEM] * 3,
        out_specs=(VMEM, VMEM),
        compiler_params=params(16),
        cost_estimate=SMALL,
        name="project_images",
    )(images, key_weight, value_weight)


def attend_kernel(key_rows, far_count, chunk, slots, own, sibling, *rest):
    far = rest[:far_count]
    keys, values, query_weight, out_weight, gain = rest[far_count : far_count + 5]
    outs = rest[far_count + 5 : far_count + 5 + len(chunk)]
    rows, query, context = rest[far_count + 5 + len(chunk) :]
    column = lax.axis_index("cap")
    tokens, width = own.shape[1], own.shape[2]
    head_size = width // HEADS
    heads = GROUP // head_size
    pair_count = len(chunk) * IMG_MOST
    images = []
    for pair in range(pair_count):
        entry = slots[chunk[pair // IMG_MOST] * IMG_MOST + pair % IMG_MOST]
        image, owner, local = split_entry(entry, own.shape[0])
        images.append(image)
        apart = jnp.bitwise_xor(owner, column)

        @pl.when(apart == 0)
        def _():
            rows[pair] = own[local]

        @pl.when(apart == 1)
        def _():
            rows[pair] = sibling[local]

        for step in range(far_count):

            @pl.when(apart // CORES == step + 1)
            def _():
                rows[pair] = far[step][pair]

    flat = rows[...].reshape(pair_count * tokens, width)
    query[...] = jnp.dot(flat, query_weight[...], preferred_element_type=F32).astype(BF16)
    lane_head = lax.broadcasted_iota(jnp.int32, (tokens, GROUP), 1) // head_size
    visible = lax.broadcasted_iota(jnp.int32, (heads * tokens, KEY_PAD), 1) < key_rows
    scale = 1.0 / float(head_size) ** 0.5
    spans = [slice(group * GROUP, (group + 1) * GROUP) for group in range(width // GROUP)]

    def score(pair):
        found = []
        for span in spans:
            part = query[pair * tokens : (pair + 1) * tokens, span]
            stacked = jnp.concatenate(
                [jnp.where(lane_head == head, part, jnp.zeros_like(part)) for head in range(heads)],
                axis=0,
            )
            found.append(
                lax.dot_general(
                    stacked,
                    keys[images[pair], :, span],
                    (((1,), (1,)), ((), ())),
                    preferred_element_type=F32,
                )
            )
        return found

    def mix(pair, found):
        for span, scores in zip(spans, found):
            scores = jnp.where(visible, scores * scale, -jnp.inf)
            top = jnp.max(scores, axis=-1, keepdims=True)
            weights = jnp.exp(scores - top)
            share = 1.0 / jnp.sum(weights, axis=-1, keepdims=True)
            probs = (weights * share).astype(BF16)
            mixed = jnp.dot(probs, values[images[pair], :, span], preferred_element_type=F32)
            joined = mixed[:tokens]
            for head in range(1, heads):
                joined = jnp.where(lane_head == head, mixed[head * tokens : (head + 1) * tokens], joined)
            context[pair * tokens : (pair + 1) * tokens, span] = joined.astype(BF16)

    every = [score(pair) for pair in range(pair_count)]
    for pair in range(pair_count):
        mix(pair, every[pair])
    hidden = flat.astype(F32) + jnp.dot(context[...], out_weight[...], preferred_element_type=F32)
    hidden = norm_rows(hidden, gain[...]).astype(BF16).reshape(pair_count, tokens, width)
    for index, out in enumerate(outs):
        out[...] = hidden[index * IMG_MOST : (index + 1) * IMG_MOST]


def attend(key_rows, chunk, slots, own, sibling, far, keys, values, query_weight, out_weight, gain):
    tokens, width = own.shape[1:]
    pair_count = len(chunk) * IMG_MOST
    rows = pair_count * tokens
    return pl.pallas_call(
        functools.partial(attend_kernel, key_rows, len(far), chunk),
        out_shape=(jax.ShapeDtypeStruct((IMG_MOST, tokens, width), BF16),) * len(chunk),
        in_specs=[SMEM] + [VMEM] * (7 + len(far)),
        out_specs=(VMEM,) * len(chunk),
        scratch_shapes=[
            pltpu.VMEM((pair_count, tokens, width), BF16),
            pltpu.VMEM((rows, width), BF16),
            pltpu.VMEM((rows, width), BF16),
        ],
        compiler_params=params(16),
        cost_estimate=SMALL,
        name="attend",
    )(slots, own, sibling, *far, keys, values, query_weight, out_weight, gain)


TILES = 3


def feed_rows(parts, gain, in_weight, back_weight):
    count, tokens, width = parts[0].shape
    step = in_weight.shape[1] // TILES
    flat = jnp.concatenate([part[...] for part in parts], axis=0).reshape(-1, width)
    total = flat.astype(F32)
    for tile in range(TILES):
        span = slice(tile * step, (tile + 1) * step)
        inner = jnp.dot(flat, in_weight[:, span], preferred_element_type=F32)
        inner = (0.5 * inner * (1.0 + lax.erf(inner * (0.5**0.5)))).astype(BF16)
        total = total + jnp.dot(inner, back_weight[span, :], preferred_element_type=F32)
    return norm_rows(total, gain[...]).astype(BF16).reshape(-1, tokens, width)


def feed_first_kernel(gain, in_weight, back_weight, *rest):
    parts, out = rest[:-1], rest[-1]
    out[...] = feed_rows(parts, gain, in_weight, back_weight)


def feed_last_kernel(first_parts, last_parts, place, gain, match_weight, in_weight, back_weight, earlier, *rest):
    parts = rest[: len(last_parts)]
    merged, logits, done, first = rest[len(last_parts) :]
    slots = len(first_parts) * IMG_MOST
    done[:slots] = earlier[...]
    done[slots:] = feed_rows(parts, gain, in_weight, back_weight)
    for row in range(merged.shape[0]):
        slot = place[row]
        distance = slot // IMG_MOST
        spot = jnp.int32(0)
        for index, listed in enumerate(first_parts + last_parts):
            spot = jnp.where(distance == listed, index, spot)
        block = done[spot * IMG_MOST + slot % IMG_MOST]
        merged[row] = block
        first[row : row + 1, :] = block[0:1, :].astype(F32)
    logits[...] = lax.dot_general(
        match_weight[...], first[...].astype(BF16), (((1,), (1,)), ((), ())), preferred_element_type=F32
    )


def feed_cost(rows, width, inner_width):
    return pl.CostEstimate(
        flops=4 * rows * width * inner_width,
        bytes_accessed=4 * width * inner_width,
        transcendentals=rows * inner_width,
    )


def feed_first(parts, gain, in_weight, back_weight):
    count, tokens, width = parts[0].shape
    slots = len(parts) * count
    return pl.pallas_call(
        feed_first_kernel,
        out_shape=jax.ShapeDtypeStruct((slots, tokens, width), BF16),
        in_specs=[VMEM] * (3 + len(parts)),
        out_specs=VMEM,
        compiler_params=params(16),
        cost_estimate=feed_cost(slots * tokens, width, in_weight.shape[1]),
        name="feed_first",
    )(gain, in_weight, back_weight, *parts)


def feed_last(first_parts, last_parts, place, gain, match_weight, in_weight, back_weight, earlier, parts):
    count, tokens, width = parts[0].shape
    rows = place.shape[0]
    slots = (len(first_parts) + len(last_parts)) * count
    return pl.pallas_call(
        functools.partial(feed_last_kernel, first_parts, last_parts),
        out_shape=(
            jax.ShapeDtypeStruct((rows, tokens, width), BF16),
            jax.ShapeDtypeStruct((match_weight.shape[0], rows), F32),
        ),
        in_specs=[SMEM] + [VMEM] * (5 + len(parts)),
        out_specs=(VMEM, VMEM),
        scratch_shapes=[pltpu.VMEM((slots, tokens, width), BF16), pltpu.VMEM((rows, width), F32)],
        compiler_params=params(16),
        cost_estimate=feed_cost(len(parts) * count * tokens, width, in_weight.shape[1]),
        name="feed_last",
    )(place, gain, match_weight, in_weight, back_weight, earlier, *parts)


def body(
    pair_list,
    verify_order,
    image_slot,
    caption_slot,
    images,
    captions,
    query_weight,
    key_weight,
    value_weight,
    out_weight,
    gain_attn,
    in_weight,
    back_weight,
    gain_ffn,
    match_weight,
):
    img_count = lax.axis_size("img")
    cap_count = lax.axis_size("cap")
    far_steps = range(1, cap_count // CORES)
    half = img_count // 2
    chunks = tuple((img_count - 1 - index, index) for index in range(half))
    first_parts = sum(chunks[: half // 2], ())
    last_parts = sum(chunks[half // 2 :], ())

    def swap(array, axis, distance):
        size = lax.axis_size(axis)
        return lax.ppermute(array, axis, [(peer, peer ^ distance) for peer in range(size)])

    sibling = swap(captions, "cap", 1)
    table, place = make_table(
        pair_list.T, verify_order, image_slot, caption_slot, images.shape[0], img_count, cap_count
    )
    table = lax.all_to_all(table, ("img", "cap"), split_axis=0, concat_axis=0, tiled=True)
    keys, values = project_images(images, key_weight, value_weight)
    pinned = pltpu.with_memory_space_constraint(captions, pltpu.HBM)
    far = [[] for _ in chunks]
    for step in far_steps:
        slots, *picked = pick_blocks(step, cap_count, chunks, table, pinned, sibling)
        for blocks, block in zip(far, picked):
            blocks.append(block)
    gain_attn = gain_attn.reshape(1, -1)
    gain_ffn = gain_ffn.reshape(1, -1)
    hidden = {}

    def after(value, parts):
        value, found = lax.optimization_barrier((value, [hidden[part] for part in parts]))
        hidden.update(zip(parts, found))
        return value

    def fetch(index):
        far[index] = [swap(block, "cap", step * CORES) for step, block in zip(far_steps, far[index])]

    fetch(0)
    fetch(1)
    for index, chunk in enumerate(chunks):
        if index >= 2:
            slots = after(slots, chunks[index - 2])
        blocks = attend(
            images.shape[1],
            chunk,
            slots,
            captions,
            sibling,
            far[index],
            keys,
            values,
            query_weight,
            out_weight,
            gain_attn,
        )
        if index == 0:
            blocks, far[2:] = lax.optimization_barrier((blocks, far[2:]))
            for later in range(2, len(chunks)):
                fetch(later)
        for distance, block in zip(chunk, blocks):
            hidden[distance] = swap(block, "img", distance) if distance else block
    gain_ffn = after(gain_ffn, sum(chunks[:-1], ()))
    earlier = feed_first([hidden[part] for part in first_parts], gain_ffn, in_weight, back_weight)
    merged, logits = feed_last(
        first_parts,
        last_parts,
        place,
        gain_ffn,
        match_weight.T,
        in_weight,
        back_weight,
        earlier,
        [hidden[part] for part in last_parts],
    )
    return merged, logits.T


def solution(mesh):
    placed = (
        P(),
        P(("img", "cap")),
        P(),
        P(),
        P("img", None, None),
        P("cap", None, None),
        P(),
        P(),
        P(),
        P(),
        P(),
        P(),
        P(),
        P(),
        P(),
    )
    return jax.shard_map(
        body,
        mesh=mesh,
        in_specs=placed,
        out_specs=(P(("img", "cap"), None, None), P(("img", "cap"), None)),
        check_vma=False,
    )
```

```python
import functools

import jax
import jax.numpy as jnp
from jax import lax
from jax.experimental import pallas as pl
from jax.experimental.pallas import tpu as pltpu
from jax.sharding import PartitionSpec as P

HEADS = 12
IMG_MOST = 2
PIECES = 4
CORES = 2
PACK = 65536
KEY_PAD = 256
LANES = 128
GROUP = 256
F32 = jnp.float32
BF16 = jnp.bfloat16
SMALL = pl.CostEstimate(flops=1 << 16, bytes_accessed=1 << 10, transcendentals=0)

SMEM = pl.BlockSpec(memory_space=pltpu.SMEM)
VMEM = pl.BlockSpec(memory_space=pltpu.VMEM)
ANY = pl.BlockSpec(memory_space=pl.ANY)


def params(mib):
    return pltpu.CompilerParams(vmem_limit_bytes=mib * 1024 * 1024)


def norm_rows(hidden, gain):
    row_mean = jnp.mean(hidden, axis=-1, keepdims=True)
    centred = hidden - row_mean
    row_var = jnp.mean(centred * centred, axis=-1, keepdims=True)
    return centred * lax.rsqrt(row_var + 1e-06) * gain


def table_kernel(image_local, caption_count, pairs, order, image_slot, caption_slot, table, place, count):
    img_count = count.shape[0]
    me = lax.axis_index("img")
    for owner in range(img_count):
        count[owner] = 0
        for rank in range(IMG_MOST if img_count * IMG_MOST > order.shape[0] else 0):
            for column in range(caption_count):
                table[owner * caption_count + column, rank] = 0
    for row in range(order.shape[0]):
        pair = order[row]
        image = image_slot[pairs[0, pair]]
        caption = caption_slot[pairs[1, pair]]
        owner = image // image_local
        rank = count[owner]
        count[owner] = rank + 1
        entry = (image - owner * image_local) * PACK + caption
        for column in range(caption_count):
            table[owner * caption_count + column, rank] = entry
        place[row] = jnp.bitwise_xor(owner, me) * IMG_MOST + rank


def make_table(pairs, order, image_slot, caption_slot, image_local, img_count, caption_count):
    return pl.pallas_call(
        functools.partial(table_kernel, image_local, caption_count),
        out_shape=(
            jax.ShapeDtypeStruct((img_count * caption_count, LANES), jnp.int32),
            jax.ShapeDtypeStruct(order.shape, jnp.int32),
        ),
        in_specs=[SMEM] * 4,
        out_specs=(SMEM, SMEM),
        scratch_shapes=[pltpu.SMEM((img_count,), jnp.int32)],
        name="slot_table",
    )(pairs, order, image_slot, caption_slot)


def split_entry(entry, caption_local):
    caption = jnp.bitwise_and(entry, PACK - 1)
    owner = caption // caption_local
    return lax.shift_right_logical(entry, 16), owner, caption - owner * caption_local


def pick_kernel(step, cap_count, chunks, table, captions, sibling, slots, *rest):
    outs, own, sems = rest[: len(chunks)], rest[len(chunks)], rest[len(chunks) + 1]
    piece = own.shape[0] // PIECES
    copies = []
    for index in range(PIECES):
        span = pl.ds(index * piece, piece)
        copies.append(pltpu.make_async_copy(captions.at[span], own.at[span], sems.at[index]))
        copies[-1].start()
    me = lax.axis_index("img")
    mine = lax.axis_index("cap")
    asker = jnp.bitwise_xor(mine, step * CORES)
    picks = []
    for chunk, out in zip(chunks, outs):
        for index, distance in enumerate(chunk):
            verifier = jnp.bitwise_xor(me, distance) * cap_count
            for rank in range(IMG_MOST):
                slots[distance * IMG_MOST + rank] = table[verifier + mine, rank]
                _, owner, local = split_entry(table[verifier + asker, rank], own.shape[0])
                near = owner == jnp.bitwise_xor(mine, 1)
                picks.append((out, index * IMG_MOST + rank, near, local))

                @pl.when(near)
                def _():
                    out[index * IMG_MOST + rank] = sibling[local]

    for copy in copies:
        copy.wait()
    for out, spot, near, local in picks:

        @pl.when(jnp.logical_not(near))
        def _():
            out[spot] = own[local]


def pick_blocks(step, cap_count, chunks, table, own, sibling):
    slot_count = sum(len(chunk) for chunk in chunks) * IMG_MOST
    outs = tuple(
        jax.ShapeDtypeStruct((len(chunk) * IMG_MOST,) + own.shape[1:], own.dtype) for chunk in chunks
    )
    return pl.pallas_call(
        functools.partial(pick_kernel, step, cap_count, chunks),
        out_shape=(jax.ShapeDtypeStruct((slot_count,), jnp.int32),) + outs,
        in_specs=[SMEM, ANY, VMEM],
        out_specs=(SMEM,) + (VMEM,) * len(outs),
        scratch_shapes=[pltpu.VMEM(own.shape, own.dtype), pltpu.SemaphoreType.DMA((PIECES,))],
        compiler_params=params(8),
        cost_estimate=SMALL,
        name="pick_captions",
    )(table, own, sibling)


def project_kernel(images, weight, out):
    count, rows, width = images.shape
    whole = rows // 16 * 16
    for image in range(count):
        out[image, whole:, :] = jnp.zeros((KEY_PAD - whole, width), BF16)
        out[image, :rows, :] = jnp.dot(images[image], weight[...], preferred_element_type=F32).astype(BF16)


def project_images(images, weight):
    count, rows, width = images.shape
    return pl.pallas_call(
        project_kernel,
        out_shape=jax.ShapeDtypeStruct((count, KEY_PAD, width), BF16),
        in_specs=[VMEM] * 2,
        out_specs=VMEM,
        compiler_params=params(16),
        cost_estimate=SMALL,
        name="project_images",
    )(images, weight)


def attend_kernel(key_rows, far_count, chunk, slots, own, sibling, *rest):
    far = rest[:far_count]
    keys, values, query_weight, out_weight, gain = rest[far_count : far_count + 5]
    outs = rest[far_count + 5 : far_count + 5 + len(chunk)]
    rows, query, context = rest[far_count + 5 + len(chunk) :]
    column = lax.axis_index("cap")
    tokens, width = own.shape[1], own.shape[2]
    head_size = width // HEADS
    heads = GROUP // head_size
    pair_count = len(chunk) * IMG_MOST
    images = []
    for pair in range(pair_count):
        entry = slots[chunk[pair // IMG_MOST] * IMG_MOST + pair % IMG_MOST]
        image, owner, local = split_entry(entry, own.shape[0])
        images.append(image)
        apart = jnp.bitwise_xor(owner, column)

        @pl.when(apart == 0)
        def _():
            rows[pair] = own[local]

        @pl.when(apart == 1)
        def _():
            rows[pair] = sibling[local]

        for step in range(far_count):

            @pl.when(apart // CORES == step + 1)
            def _():
                rows[pair] = far[step][pair]

    flat = rows[...].reshape(pair_count * tokens, width)
    query[...] = jnp.dot(flat, query_weight[...], preferred_element_type=F32).astype(BF16)
    lane_head = lax.broadcasted_iota(jnp.int32, (tokens, GROUP), 1) // head_size
    visible = lax.broadcasted_iota(jnp.int32, (heads * tokens, KEY_PAD), 1) < key_rows
    scale = 1.0 / float(head_size) ** 0.5
    spans = [slice(group * GROUP, (group + 1) * GROUP) for group in range(width // GROUP)]

    def score(pair):
        found = []
        for span in spans:
            part = query[pair * tokens : (pair + 1) * tokens, span]
            stacked = jnp.concatenate(
                [jnp.where(lane_head == head, part, jnp.zeros_like(part)) for head in range(heads)],
                axis=0,
            )
            found.append(
                lax.dot_general(
                    stacked,
                    keys[images[pair], :, span],
                    (((1,), (1,)), ((), ())),
                    preferred_element_type=F32,
                )
            )
        return found

    def mix(pair, found):
        for span, scores in zip(spans, found):
            scores = jnp.where(visible, scores * scale, -jnp.inf)
            top = jnp.max(scores, axis=-1, keepdims=True)
            weights = jnp.exp(scores - top)
            share = 1.0 / jnp.sum(weights, axis=-1, keepdims=True)
            probs = (weights * share).astype(BF16)
            mixed = jnp.dot(probs, values[images[pair], :, span], preferred_element_type=F32)
            joined = mixed[:tokens]
            for head in range(1, heads):
                joined = jnp.where(lane_head == head, mixed[head * tokens : (head + 1) * tokens], joined)
            context[pair * tokens : (pair + 1) * tokens, span] = joined.astype(BF16)

    every = [score(pair) for pair in range(pair_count)]
    for pair in range(pair_count):
        mix(pair, every[pair])
    hidden = flat.astype(F32) + jnp.dot(context[...], out_weight[...], preferred_element_type=F32)
    hidden = norm_rows(hidden, gain[...]).astype(BF16).reshape(pair_count, tokens, width)
    for index, out in enumerate(outs):
        out[...] = hidden[index * IMG_MOST : (index + 1) * IMG_MOST]


def attend(key_rows, chunk, slots, own, sibling, far, keys, values, query_weight, out_weight, gain):
    tokens, width = own.shape[1:]
    pair_count = len(chunk) * IMG_MOST
    rows = pair_count * tokens
    return pl.pallas_call(
        functools.partial(attend_kernel, key_rows, len(far), chunk),
        out_shape=(jax.ShapeDtypeStruct((IMG_MOST, tokens, width), BF16),) * len(chunk),
        in_specs=[SMEM] + [VMEM] * (7 + len(far)),
        out_specs=(VMEM,) * len(chunk),
        scratch_shapes=[
            pltpu.VMEM((pair_count, tokens, width), BF16),
            pltpu.VMEM((rows, width), BF16),
            pltpu.VMEM((rows, width), BF16),
        ],
        compiler_params=params(16),
        cost_estimate=SMALL,
        name="attend",
    )(slots, own, sibling, *far, keys, values, query_weight, out_weight, gain)


TILES = 3


def feed_rows(parts, gain, in_weight, back_weight):
    count, tokens, width = parts[0].shape
    step = in_weight.shape[1] // TILES
    flat = jnp.concatenate([part[...] for part in parts], axis=0).reshape(-1, width)
    total = flat.astype(F32)
    for tile in range(TILES):
        span = slice(tile * step, (tile + 1) * step)
        inner = jnp.dot(flat, in_weight[:, span], preferred_element_type=F32)
        inner = (0.5 * inner * (1.0 + lax.erf(inner * (0.5**0.5)))).astype(BF16)
        total = total + jnp.dot(inner, back_weight[span, :], preferred_element_type=F32)
    return norm_rows(total, gain[...]).astype(BF16).reshape(-1, tokens, width)


def feed_first_kernel(gain, in_weight, back_weight, *rest):
    parts, out = rest[:-1], rest[-1]
    out[...] = feed_rows(parts, gain, in_weight, back_weight)


def feed_last_kernel(first_parts, last_parts, place, gain, match_weight, in_weight, back_weight, earlier, *rest):
    parts = rest[: len(last_parts)]
    merged, logits, done, first = rest[len(last_parts) :]
    slots = len(first_parts) * IMG_MOST
    done[:slots] = earlier[...]
    done[slots:] = feed_rows(parts, gain, in_weight, back_weight)
    for row in range(merged.shape[0]):
        slot = place[row]
        distance = slot // IMG_MOST
        spot = jnp.int32(0)
        for index, listed in enumerate(first_parts + last_parts):
            spot = jnp.where(distance == listed, index, spot)
        block = done[spot * IMG_MOST + slot % IMG_MOST]
        merged[row] = block
        first[row : row + 1, :] = block[0:1, :].astype(F32)
    logits[...] = lax.dot_general(
        match_weight[...], first[...].astype(BF16), (((1,), (1,)), ((), ())), preferred_element_type=F32
    )


def feed_cost(rows, width, inner_width):
    return pl.CostEstimate(
        flops=4 * rows * width * inner_width,
        bytes_accessed=4 * width * inner_width,
        transcendentals=rows * inner_width,
    )


def feed_first(parts, gain, in_weight, back_weight):
    count, tokens, width = parts[0].shape
    slots = len(parts) * count
    return pl.pallas_call(
        feed_first_kernel,
        out_shape=jax.ShapeDtypeStruct((slots, tokens, width), BF16),
        in_specs=[VMEM] * (3 + len(parts)),
        out_specs=VMEM,
        compiler_params=params(16),
        cost_estimate=feed_cost(slots * tokens, width, in_weight.shape[1]),
        name="feed_first",
    )(gain, in_weight, back_weight, *parts)


def feed_last(first_parts, last_parts, place, gain, match_weight, in_weight, back_weight, earlier, parts):
    count, tokens, width = parts[0].shape
    rows = place.shape[0]
    slots = (len(first_parts) + len(last_parts)) * count
    return pl.pallas_call(
        functools.partial(feed_last_kernel, first_parts, last_parts),
        out_shape=(
            jax.ShapeDtypeStruct((rows, tokens, width), BF16),
            jax.ShapeDtypeStruct((match_weight.shape[0], rows), F32),
        ),
        in_specs=[SMEM] + [VMEM] * (5 + len(parts)),
        out_specs=(VMEM, VMEM),
        scratch_shapes=[pltpu.VMEM((slots, tokens, width), BF16), pltpu.VMEM((rows, width), F32)],
        compiler_params=params(16),
        cost_estimate=feed_cost(len(parts) * count * tokens, width, in_weight.shape[1]),
        name="feed_last",
    )(place, gain, match_weight, in_weight, back_weight, earlier, *parts)


def body(
    pair_list,
    verify_order,
    image_slot,
    caption_slot,
    images,
    captions,
    query_weight,
    key_weight,
    value_weight,
    out_weight,
    gain_attn,
    in_weight,
    back_weight,
    gain_ffn,
    match_weight,
):
    img_count = lax.axis_size("img")
    cap_count = lax.axis_size("cap")
    far_steps = range(1, cap_count // CORES)
    half = img_count // 2
    chunks = tuple((img_count - 1 - index, index) for index in range(half))
    first_parts = sum(chunks[: half // 2], ())
    last_parts = sum(chunks[half // 2 :], ())

    def swap(array, axis, distance):
        size = lax.axis_size(axis)
        return lax.ppermute(array, axis, [(peer, peer ^ distance) for peer in range(size)])

    sibling = swap(captions, "cap", 1)
    table, place = make_table(
        pair_list.T, verify_order, image_slot, caption_slot, images.shape[0], img_count, cap_count
    )
    table = lax.all_to_all(table, ("img", "cap"), split_axis=0, concat_axis=0, tiled=True)
    keys = project_images(images, key_weight)
    value_weight, keys = lax.optimization_barrier((value_weight, keys))
    values = project_images(images, value_weight)
    pinned = pltpu.with_memory_space_constraint(captions, pltpu.HBM)
    far = [[] for _ in chunks]
    for step in far_steps:
        slots, *picked = pick_blocks(step, cap_count, chunks, table, pinned, sibling)
        for blocks, block in zip(far, picked):
            blocks.append(block)
    gain_attn = gain_attn.reshape(1, -1)
    gain_ffn = gain_ffn.reshape(1, -1)
    hidden = {}

    def after(value, parts):
        value, found = lax.optimization_barrier((value, [hidden[part] for part in parts]))
        hidden.update(zip(parts, found))
        return value

    def fetch(index):
        far[index] = [swap(block, "cap", step * CORES) for step, block in zip(far_steps, far[index])]

    fetch(0)
    far[1], keys = lax.optimization_barrier((far[1], keys))
    fetch(1)
    far[2:], values = lax.optimization_barrier((far[2:], values))
    for later in range(2, len(chunks)):
        fetch(later)
    for index, chunk in enumerate(chunks):
        if index >= 2:
            slots = after(slots, chunks[index - 2])
        blocks = attend(
            images.shape[1],
            chunk,
            slots,
            captions,
            sibling,
            far[index],
            keys,
            values,
            query_weight,
            out_weight,
            gain_attn,
        )
        for distance, block in zip(chunk, blocks):
            hidden[distance] = swap(block, "img", distance) if distance else block
    gain_ffn = after(gain_ffn, sum(chunks[:-1], ()))
    earlier = feed_first([hidden[part] for part in first_parts], gain_ffn, in_weight, back_weight)
    merged, logits = feed_last(
        first_parts,
        last_parts,
        place,
        gain_ffn,
        match_weight.T,
        in_weight,
        back_weight,
        earlier,
        [hidden[part] for part in last_parts],
    )
    return merged, logits.T


def solution(mesh):
    placed = (
        P(),
        P(("img", "cap")),
        P(),
        P(),
        P("img", None, None),
        P("cap", None, None),
        P(),
        P(),
        P(),
        P(),
        P(),
        P(),
        P(),
        P(),
        P(),
    )
    return jax.shard_map(
        body,
        mesh=mesh,
        in_specs=placed,
        out_specs=(P(("img", "cap"), None, None), P(("img", "cap"), None)),
        check_vma=False,
    )
```

```python
import functools

import jax
import jax.numpy as jnp
from jax import lax
from jax.experimental import pallas as pl
from jax.experimental.pallas import tpu as pltpu
from jax.sharding import PartitionSpec as P

HEADS = 12
IMG_MOST = 2
PIECES = 4
CORES = 2
PACK = 65536
KEY_PAD = 256
LANES = 128
GROUP = 256
F32 = jnp.float32
BF16 = jnp.bfloat16
SMALL = pl.CostEstimate(flops=1 << 16, bytes_accessed=1 << 10, transcendentals=0)

SMEM = pl.BlockSpec(memory_space=pltpu.SMEM)
VMEM = pl.BlockSpec(memory_space=pltpu.VMEM)
ANY = pl.BlockSpec(memory_space=pl.ANY)


def params(mib):
    return pltpu.CompilerParams(vmem_limit_bytes=mib * 1024 * 1024)


def norm_rows(hidden, gain):
    row_mean = jnp.mean(hidden, axis=-1, keepdims=True)
    centred = hidden - row_mean
    row_var = jnp.mean(centred * centred, axis=-1, keepdims=True)
    return centred * lax.rsqrt(row_var + 1e-06) * gain


def table_kernel(image_local, caption_count, pairs, order, image_slot, caption_slot, table, place, count):
    img_count = count.shape[0]
    me = lax.axis_index("img")
    for owner in range(img_count):
        count[owner] = 0
        for rank in range(IMG_MOST if img_count * IMG_MOST > order.shape[0] else 0):
            for column in range(caption_count):
                table[owner * caption_count + column, rank] = 0
    for row in range(order.shape[0]):
        pair = order[row]
        image = image_slot[pairs[0, pair]]
        caption = caption_slot[pairs[1, pair]]
        owner = image // image_local
        rank = count[owner]
        count[owner] = rank + 1
        entry = (image - owner * image_local) * PACK + caption
        for column in range(caption_count):
            table[owner * caption_count + column, rank] = entry
        place[row] = jnp.bitwise_xor(owner, me) * IMG_MOST + rank


def make_table(pairs, order, image_slot, caption_slot, image_local, img_count, caption_count):
    return pl.pallas_call(
        functools.partial(table_kernel, image_local, caption_count),
        out_shape=(
            jax.ShapeDtypeStruct((img_count * caption_count, LANES), jnp.int32),
            jax.ShapeDtypeStruct(order.shape, jnp.int32),
        ),
        in_specs=[SMEM] * 4,
        out_specs=(SMEM, SMEM),
        scratch_shapes=[pltpu.SMEM((img_count,), jnp.int32)],
        name="slot_table",
    )(pairs, order, image_slot, caption_slot)


def split_entry(entry, caption_local):
    caption = jnp.bitwise_and(entry, PACK - 1)
    owner = caption // caption_local
    return lax.shift_right_logical(entry, 16), owner, caption - owner * caption_local


def pick_kernel(step, cap_count, chunks, table, captions, sibling, slots, *rest):
    outs, own, sems = rest[: len(chunks)], rest[len(chunks)], rest[len(chunks) + 1]
    piece = own.shape[0] // PIECES
    copies = []
    for index in range(PIECES):
        span = pl.ds(index * piece, piece)
        copies.append(pltpu.make_async_copy(captions.at[span], own.at[span], sems.at[index]))
        copies[-1].start()
    me = lax.axis_index("img")
    mine = lax.axis_index("cap")
    asker = jnp.bitwise_xor(mine, step * CORES)
    picks = []
    for chunk, out in zip(chunks, outs):
        for index, distance in enumerate(chunk):
            verifier = jnp.bitwise_xor(me, distance) * cap_count
            for rank in range(IMG_MOST):
                slots[distance * IMG_MOST + rank] = table[verifier + mine, rank]
                _, owner, local = split_entry(table[verifier + asker, rank], own.shape[0])
                near = owner == jnp.bitwise_xor(mine, 1)
                picks.append((out, index * IMG_MOST + rank, near, local))

                @pl.when(near)
                def _():
                    out[index * IMG_MOST + rank] = sibling[local]

    for copy in copies:
        copy.wait()
    for out, spot, near, local in picks:

        @pl.when(jnp.logical_not(near))
        def _():
            out[spot] = own[local]


def pick_blocks(step, cap_count, chunks, table, own, sibling):
    slot_count = sum(len(chunk) for chunk in chunks) * IMG_MOST
    outs = tuple(
        jax.ShapeDtypeStruct((len(chunk) * IMG_MOST,) + own.shape[1:], own.dtype) for chunk in chunks
    )
    return pl.pallas_call(
        functools.partial(pick_kernel, step, cap_count, chunks),
        out_shape=(jax.ShapeDtypeStruct((slot_count,), jnp.int32),) + outs,
        in_specs=[SMEM, ANY, VMEM],
        out_specs=(SMEM,) + (VMEM,) * len(outs),
        scratch_shapes=[pltpu.VMEM(own.shape, own.dtype), pltpu.SemaphoreType.DMA((PIECES,))],
        compiler_params=params(8),
        cost_estimate=SMALL,
        name="pick_captions",
    )(table, own, sibling)


def project_kernel(images, weight, out):
    count, rows, width = images.shape
    whole = rows // 16 * 16
    for image in range(count):
        out[image, whole:, :] = jnp.zeros((KEY_PAD - whole, width), BF16)
        out[image, :rows, :] = jnp.dot(images[image], weight[...], preferred_element_type=F32).astype(BF16)


def project_images(images, weight):
    count, rows, width = images.shape
    return pl.pallas_call(
        project_kernel,
        out_shape=jax.ShapeDtypeStruct((count, KEY_PAD, width), BF16),
        in_specs=[VMEM] * 2,
        out_specs=VMEM,
        compiler_params=params(16),
        cost_estimate=SMALL,
        name="project_images",
    )(images, weight)


def attend_kernel(key_rows, far_count, chunk, slots, own, sibling, *rest):
    far = rest[:far_count]
    keys, values, query_weight, out_weight, gain = rest[far_count : far_count + 5]
    outs = rest[far_count + 5 : far_count + 5 + len(chunk)]
    rows, query, context = rest[far_count + 5 + len(chunk) :]
    column = lax.axis_index("cap")
    tokens, width = own.shape[1], own.shape[2]
    head_size = width // HEADS
    heads = GROUP // head_size
    pair_count = len(chunk) * IMG_MOST
    images = []
    for pair in range(pair_count):
        entry = slots[chunk[pair // IMG_MOST] * IMG_MOST + pair % IMG_MOST]
        image, owner, local = split_entry(entry, own.shape[0])
        images.append(image)
        apart = jnp.bitwise_xor(owner, column)

        @pl.when(apart == 0)
        def _():
            rows[pair] = own[local]

        @pl.when(apart == 1)
        def _():
            rows[pair] = sibling[local]

        for step in range(far_count):

            @pl.when(apart // CORES == step + 1)
            def _():
                rows[pair] = far[step][pair]

    flat = rows[...].reshape(pair_count * tokens, width)
    query[...] = jnp.dot(flat, query_weight[...], preferred_element_type=F32).astype(BF16)
    lane_head = lax.broadcasted_iota(jnp.int32, (tokens, GROUP), 1) // head_size
    visible = lax.broadcasted_iota(jnp.int32, (heads * tokens, KEY_PAD), 1) < key_rows
    scale = 1.0 / float(head_size) ** 0.5
    spans = [slice(group * GROUP, (group + 1) * GROUP) for group in range(width // GROUP)]

    def score(pair):
        found = []
        for span in spans:
            part = query[pair * tokens : (pair + 1) * tokens, span]
            stacked = jnp.concatenate(
                [jnp.where(lane_head == head, part, jnp.zeros_like(part)) for head in range(heads)],
                axis=0,
            )
            found.append(
                lax.dot_general(
                    stacked,
                    keys[images[pair], :, span],
                    (((1,), (1,)), ((), ())),
                    preferred_element_type=F32,
                )
            )
        return found

    def mix(pair, found):
        for span, scores in zip(spans, found):
            scores = jnp.where(visible, scores * scale, -jnp.inf)
            top = jnp.max(scores, axis=-1, keepdims=True)
            weights = jnp.exp(scores - top)
            share = 1.0 / jnp.sum(weights, axis=-1, keepdims=True)
            probs = (weights * share).astype(BF16)
            mixed = jnp.dot(probs, values[images[pair], :, span], preferred_element_type=F32)
            joined = mixed[:tokens]
            for head in range(1, heads):
                joined = jnp.where(lane_head == head, mixed[head * tokens : (head + 1) * tokens], joined)
            context[pair * tokens : (pair + 1) * tokens, span] = joined.astype(BF16)

    every = [score(pair) for pair in range(pair_count)]
    for pair in range(pair_count):
        mix(pair, every[pair])
    hidden = flat.astype(F32) + jnp.dot(context[...], out_weight[...], preferred_element_type=F32)
    hidden = norm_rows(hidden, gain[...]).astype(BF16).reshape(pair_count, tokens, width)
    for index, out in enumerate(outs):
        out[...] = hidden[index * IMG_MOST : (index + 1) * IMG_MOST]


def attend(key_rows, chunk, slots, own, sibling, far, keys, values, query_weight, out_weight, gain):
    tokens, width = own.shape[1:]
    pair_count = len(chunk) * IMG_MOST
    rows = pair_count * tokens
    return pl.pallas_call(
        functools.partial(attend_kernel, key_rows, len(far), chunk),
        out_shape=(jax.ShapeDtypeStruct((IMG_MOST, tokens, width), BF16),) * len(chunk),
        in_specs=[SMEM] + [VMEM] * (7 + len(far)),
        out_specs=(VMEM,) * len(chunk),
        scratch_shapes=[
            pltpu.VMEM((pair_count, tokens, width), BF16),
            pltpu.VMEM((rows, width), BF16),
            pltpu.VMEM((rows, width), BF16),
        ],
        compiler_params=params(16),
        cost_estimate=SMALL,
        name="attend",
    )(slots, own, sibling, *far, keys, values, query_weight, out_weight, gain)


TILES = 2


def feed_rows(parts, gain, in_weight, back_weight):
    count, tokens, width = parts[0].shape
    step = in_weight.shape[1] // TILES
    flat = jnp.concatenate([part[...] for part in parts], axis=0).reshape(-1, width)
    total = flat.astype(F32)
    for tile in range(TILES):
        span = slice(tile * step, (tile + 1) * step)
        inner = jnp.dot(flat, in_weight[:, span], preferred_element_type=F32)
        inner = (0.5 * inner * (1.0 + lax.erf(inner * (0.5**0.5)))).astype(BF16)
        total = total + jnp.dot(inner, back_weight[span, :], preferred_element_type=F32)
    return norm_rows(total, gain[...]).astype(BF16).reshape(-1, tokens, width)


def feed_first_kernel(gain, in_weight, back_weight, *rest):
    parts, out = rest[:-1], rest[-1]
    out[...] = feed_rows(parts, gain, in_weight, back_weight)


def feed_last_kernel(first_parts, last_parts, place, gain, match_weight, in_weight, back_weight, earlier, *rest):
    parts = rest[: len(last_parts)]
    merged, logits, done, first = rest[len(last_parts) :]
    slots = len(first_parts) * IMG_MOST
    done[:slots] = earlier[...]
    done[slots:] = feed_rows(parts, gain, in_weight, back_weight)
    for row in range(merged.shape[0]):
        slot = place[row]
        distance = slot // IMG_MOST
        spot = jnp.int32(0)
        for index, listed in enumerate(first_parts + last_parts):
            spot = jnp.where(distance == listed, index, spot)
        block = done[spot * IMG_MOST + slot % IMG_MOST]
        merged[row] = block
        first[row : row + 1, :] = block[0:1, :].astype(F32)
    logits[...] = lax.dot_general(
        match_weight[...], first[...].astype(BF16), (((1,), (1,)), ((), ())), preferred_element_type=F32
    )


def feed_cost(rows, width, inner_width):
    return pl.CostEstimate(
        flops=4 * rows * width * inner_width,
        bytes_accessed=4 * width * inner_width,
        transcendentals=rows * inner_width,
    )


def feed_first(parts, gain, in_weight, back_weight):
    count, tokens, width = parts[0].shape
    slots = len(parts) * count
    return pl.pallas_call(
        feed_first_kernel,
        out_shape=jax.ShapeDtypeStruct((slots, tokens, width), BF16),
        in_specs=[VMEM] * (3 + len(parts)),
        out_specs=VMEM,
        compiler_params=params(16),
        cost_estimate=feed_cost(slots * tokens, width, in_weight.shape[1]),
        name="feed_first",
    )(gain, in_weight, back_weight, *parts)


def feed_last(first_parts, last_parts, place, gain, match_weight, in_weight, back_weight, earlier, parts):
    count, tokens, width = parts[0].shape
    rows = place.shape[0]
    slots = (len(first_parts) + len(last_parts)) * count
    return pl.pallas_call(
        functools.partial(feed_last_kernel, first_parts, last_parts),
        out_shape=(
            jax.ShapeDtypeStruct((rows, tokens, width), BF16),
            jax.ShapeDtypeStruct((match_weight.shape[0], rows), F32),
        ),
        in_specs=[SMEM] + [VMEM] * (5 + len(parts)),
        out_specs=(VMEM, VMEM),
        scratch_shapes=[pltpu.VMEM((slots, tokens, width), BF16), pltpu.VMEM((rows, width), F32)],
        compiler_params=params(16),
        cost_estimate=feed_cost(len(parts) * count * tokens, width, in_weight.shape[1]),
        name="feed_last",
    )(place, gain, match_weight, in_weight, back_weight, earlier, *parts)


def body(
    pair_list,
    verify_order,
    image_slot,
    caption_slot,
    images,
    captions,
    query_weight,
    key_weight,
    value_weight,
    out_weight,
    gain_attn,
    in_weight,
    back_weight,
    gain_ffn,
    match_weight,
):
    img_count = lax.axis_size("img")
    cap_count = lax.axis_size("cap")
    far_steps = range(1, cap_count // CORES)
    half = img_count // 2
    chunks = tuple((img_count - 1 - index, index) for index in range(half))
    first_parts = sum(chunks[: half // 2], ())
    last_parts = sum(chunks[half // 2 :], ())

    def swap(array, axis, distance):
        size = lax.axis_size(axis)
        return lax.ppermute(array, axis, [(peer, peer ^ distance) for peer in range(size)])

    sibling = swap(captions, "cap", 1)
    table, place = make_table(
        pair_list.T, verify_order, image_slot, caption_slot, images.shape[0], img_count, cap_count
    )
    table = lax.all_to_all(table, ("img", "cap"), split_axis=0, concat_axis=0, tiled=True)
    keys = project_images(images, key_weight)
    value_weight, keys = lax.optimization_barrier((value_weight, keys))
    values = project_images(images, value_weight)
    pinned = pltpu.with_memory_space_constraint(captions, pltpu.HBM)
    far = [[] for _ in chunks]
    for step in far_steps:
        slots, *picked = pick_blocks(step, cap_count, chunks, table, pinned, sibling)
        for blocks, block in zip(far, picked):
            blocks.append(block)
    gain_attn = gain_attn.reshape(1, -1)
    gain_ffn = gain_ffn.reshape(1, -1)
    hidden = {}

    def after(value, parts):
        value, found = lax.optimization_barrier((value, [hidden[part] for part in parts]))
        hidden.update(zip(parts, found))
        return value

    def fetch(index):
        far[index] = [swap(block, "cap", step * CORES) for step, block in zip(far_steps, far[index])]

    fetch(0)
    far[1], keys = lax.optimization_barrier((far[1], keys))
    fetch(1)
    far[2:], values = lax.optimization_barrier((far[2:], values))
    for later in range(2, len(chunks)):
        fetch(later)
    for index, chunk in enumerate(chunks):
        if index >= 2:
            slots = after(slots, chunks[index - 2])
        blocks = attend(
            images.shape[1],
            chunk,
            slots,
            captions,
            sibling,
            far[index],
            keys,
            values,
            query_weight,
            out_weight,
            gain_attn,
        )
        for distance, block in zip(chunk, blocks):
            hidden[distance] = swap(block, "img", distance) if distance else block
    gain_ffn = after(gain_ffn, sum(chunks[:-1], ()))
    earlier = feed_first([hidden[part] for part in first_parts], gain_ffn, in_weight, back_weight)
    merged, logits = feed_last(
        first_parts,
        last_parts,
        place,
        gain_ffn,
        match_weight.T,
        in_weight,
        back_weight,
        earlier,
        [hidden[part] for part in last_parts],
    )
    return merged, logits.T


def solution(mesh):
    placed = (
        P(),
        P(("img", "cap")),
        P(),
        P(),
        P("img", None, None),
        P("cap", None, None),
        P(),
        P(),
        P(),
        P(),
        P(),
        P(),
        P(),
        P(),
        P(),
    )
    return jax.shard_map(
        body,
        mesh=mesh,
        in_specs=placed,
        out_specs=(P(("img", "cap"), None, None), P(("img", "cap"), None)),
        check_vma=False,
    )
```

```python
import functools

import jax
import jax.numpy as jnp
from jax import lax
from jax.experimental import pallas as pl
from jax.experimental.pallas import tpu as pltpu
from jax.sharding import PartitionSpec as P

HEADS = 12
IMG_MOST = 2
PIECES = 4
CORES = 2
PACK = 65536
KEY_PAD = 256
LANES = 128
GROUP = 256
F32 = jnp.float32
BF16 = jnp.bfloat16
SMALL = pl.CostEstimate(flops=1 << 16, bytes_accessed=1 << 10, transcendentals=0)

SMEM = pl.BlockSpec(memory_space=pltpu.SMEM)
VMEM = pl.BlockSpec(memory_space=pltpu.VMEM)
ANY = pl.BlockSpec(memory_space=pl.ANY)


def params(mib):
    return pltpu.CompilerParams(vmem_limit_bytes=mib * 1024 * 1024)


def norm_rows(hidden, gain):
    row_mean = jnp.mean(hidden, axis=-1, keepdims=True)
    centred = hidden - row_mean
    row_var = jnp.mean(centred * centred, axis=-1, keepdims=True)
    return centred * lax.rsqrt(row_var + 1e-06) * gain


def table_kernel(image_local, caption_count, pairs, order, image_slot, caption_slot, table, place, count):
    img_count = count.shape[0]
    me = lax.axis_index("img")
    for owner in range(img_count):
        count[owner] = 0
        for rank in range(IMG_MOST if img_count * IMG_MOST > order.shape[0] else 0):
            for column in range(caption_count):
                table[owner * caption_count + column, rank] = 0
    for row in range(order.shape[0]):
        pair = order[row]
        image = image_slot[pairs[0, pair]]
        caption = caption_slot[pairs[1, pair]]
        owner = image // image_local
        rank = count[owner]
        count[owner] = rank + 1
        entry = (image - owner * image_local) * PACK + caption
        for column in range(caption_count):
            table[owner * caption_count + column, rank] = entry
        place[row] = jnp.bitwise_xor(owner, me) * IMG_MOST + rank


def make_table(pairs, order, image_slot, caption_slot, image_local, img_count, caption_count):
    return pl.pallas_call(
        functools.partial(table_kernel, image_local, caption_count),
        out_shape=(
            jax.ShapeDtypeStruct((img_count * caption_count, LANES), jnp.int32),
            jax.ShapeDtypeStruct(order.shape, jnp.int32),
        ),
        in_specs=[SMEM] * 4,
        out_specs=(SMEM, SMEM),
        scratch_shapes=[pltpu.SMEM((img_count,), jnp.int32)],
        name="slot_table",
    )(pairs, order, image_slot, caption_slot)


def split_entry(entry, caption_local):
    caption = jnp.bitwise_and(entry, PACK - 1)
    owner = caption // caption_local
    return lax.shift_right_logical(entry, 16), owner, caption - owner * caption_local


def pick_kernel(step, cap_count, chunks, table, captions, sibling, slots, *rest):
    outs, own, sems = rest[: len(chunks)], rest[len(chunks)], rest[len(chunks) + 1]
    piece = own.shape[0] // PIECES
    copies = []
    for index in range(PIECES):
        span = pl.ds(index * piece, piece)
        copies.append(pltpu.make_async_copy(captions.at[span], own.at[span], sems.at[index]))
        copies[-1].start()
    me = lax.axis_index("img")
    mine = lax.axis_index("cap")
    asker = jnp.bitwise_xor(mine, step * CORES)
    picks = []
    for chunk, out in zip(chunks, outs):
        for index, distance in enumerate(chunk):
            verifier = jnp.bitwise_xor(me, distance) * cap_count
            for rank in range(IMG_MOST):
                slots[distance * IMG_MOST + rank] = table[verifier + mine, rank]
                _, owner, local = split_entry(table[verifier + asker, rank], own.shape[0])
                near = owner == jnp.bitwise_xor(mine, 1)
                picks.append((out, index * IMG_MOST + rank, near, local))

                @pl.when(near)
                def _():
                    out[index * IMG_MOST + rank] = sibling[local]

    for copy in copies:
        copy.wait()
    for out, spot, near, local in picks:

        @pl.when(jnp.logical_not(near))
        def _():
            out[spot] = own[local]


def pick_blocks(step, cap_count, chunks, table, own, sibling):
    slot_count = sum(len(chunk) for chunk in chunks) * IMG_MOST
    outs = tuple(
        jax.ShapeDtypeStruct((len(chunk) * IMG_MOST,) + own.shape[1:], own.dtype) for chunk in chunks
    )
    return pl.pallas_call(
        functools.partial(pick_kernel, step, cap_count, chunks),
        out_shape=(jax.ShapeDtypeStruct((slot_count,), jnp.int32),) + outs,
        in_specs=[SMEM, ANY, VMEM],
        out_specs=(SMEM,) + (VMEM,) * len(outs),
        scratch_shapes=[pltpu.VMEM(own.shape, own.dtype), pltpu.SemaphoreType.DMA((PIECES,))],
        compiler_params=params(8),
        cost_estimate=SMALL,
        name="pick_captions",
    )(table, own, sibling)


def project_kernel(turned, images, weight, out):
    count, rows, width = images.shape
    whole = rows // 16 * 16
    for image in range(count):
        found = jnp.dot(images[image], weight[...], preferred_element_type=F32).astype(BF16)
        if turned:
            out[image] = jnp.concatenate([found, jnp.zeros((KEY_PAD - rows, width), BF16)], axis=0).T
        else:
            out[image, whole:, :] = jnp.zeros((KEY_PAD - whole, width), BF16)
            out[image, :rows, :] = found


def project_images(images, weight, turned):
    count, rows, width = images.shape
    shape = (count, width, KEY_PAD) if turned else (count, KEY_PAD, width)
    return pl.pallas_call(
        functools.partial(project_kernel, turned),
        out_shape=jax.ShapeDtypeStruct(shape, BF16),
        in_specs=[VMEM] * 2,
        out_specs=VMEM,
        compiler_params=params(16),
        cost_estimate=SMALL,
        name="project_images",
    )(images, weight)


def attend_kernel(key_rows, far_count, chunk, slots, own, sibling, *rest):
    far = rest[:far_count]
    keys, values, query_weight, out_weight, gain = rest[far_count : far_count + 5]
    outs = rest[far_count + 5 : far_count + 5 + len(chunk)]
    rows, query, context = rest[far_count + 5 + len(chunk) :]
    column = lax.axis_index("cap")
    tokens, width = own.shape[1], own.shape[2]
    head_size = width // HEADS
    heads = GROUP // head_size
    pair_count = len(chunk) * IMG_MOST
    images = []
    for pair in range(pair_count):
        entry = slots[chunk[pair // IMG_MOST] * IMG_MOST + pair % IMG_MOST]
        image, owner, local = split_entry(entry, own.shape[0])
        images.append(image)
        apart = jnp.bitwise_xor(owner, column)

        @pl.when(apart == 0)
        def _():
            rows[pair] = own[local]

        @pl.when(apart == 1)
        def _():
            rows[pair] = sibling[local]

        for step in range(far_count):

            @pl.when(apart // CORES == step + 1)
            def _():
                rows[pair] = far[step][pair]

    flat = rows[...].reshape(pair_count * tokens, width)
    query[...] = jnp.dot(flat, query_weight[...], preferred_element_type=F32).astype(BF16)
    lane_head = lax.broadcasted_iota(jnp.int32, (tokens, GROUP), 1) // head_size
    visible = lax.broadcasted_iota(jnp.int32, (heads * tokens, KEY_PAD), 1) < key_rows
    scale = 1.0 / float(head_size) ** 0.5
    spans = [slice(group * GROUP, (group + 1) * GROUP) for group in range(width // GROUP)]

    def score(pair):
        found = []
        for span in spans:
            part = query[pair * tokens : (pair + 1) * tokens, span]
            stacked = jnp.concatenate(
                [jnp.where(lane_head == head, part, jnp.zeros_like(part)) for head in range(heads)],
                axis=0,
            )
            found.append(
                jnp.dot(stacked, keys[images[pair], span, :], preferred_element_type=F32)
            )
        return found

    def mix(pair, found):
        for span, scores in zip(spans, found):
            scores = jnp.where(visible, scores * scale, -jnp.inf)
            top = jnp.max(scores, axis=-1, keepdims=True)
            weights = jnp.exp(scores - top)
            share = 1.0 / jnp.sum(weights, axis=-1, keepdims=True)
            mixed = jnp.dot(
                weights.astype(BF16), values[images[pair], :, span], preferred_element_type=F32
            )
            mixed = mixed * share
            joined = mixed[:tokens]
            for head in range(1, heads):
                joined = jnp.where(lane_head == head, mixed[head * tokens : (head + 1) * tokens], joined)
            context[pair * tokens : (pair + 1) * tokens, span] = joined.astype(BF16)

    every = [score(pair) for pair in range(pair_count)]
    for pair in range(pair_count):
        mix(pair, every[pair])
    hidden = flat.astype(F32) + jnp.dot(context[...], out_weight[...], preferred_element_type=F32)
    hidden = norm_rows(hidden, gain[...]).astype(BF16).reshape(pair_count, tokens, width)
    for index, out in enumerate(outs):
        out[...] = hidden[index * IMG_MOST : (index + 1) * IMG_MOST]


def attend(key_rows, chunk, slots, own, sibling, far, keys, values, query_weight, out_weight, gain):
    tokens, width = own.shape[1:]
    pair_count = len(chunk) * IMG_MOST
    rows = pair_count * tokens
    return pl.pallas_call(
        functools.partial(attend_kernel, key_rows, len(far), chunk),
        out_shape=(jax.ShapeDtypeStruct((IMG_MOST, tokens, width), BF16),) * len(chunk),
        in_specs=[SMEM] + [VMEM] * (7 + len(far)),
        out_specs=(VMEM,) * len(chunk),
        scratch_shapes=[
            pltpu.VMEM((pair_count, tokens, width), BF16),
            pltpu.VMEM((rows, width), BF16),
            pltpu.VMEM((rows, width), BF16),
        ],
        compiler_params=params(16),
        cost_estimate=SMALL,
        name="attend",
    )(slots, own, sibling, *far, keys, values, query_weight, out_weight, gain)


TILES = 2


def feed_rows(parts, gain, in_weight, back_weight):
    count, tokens, width = parts[0].shape
    step = in_weight.shape[1] // TILES
    flat = jnp.concatenate([part[...] for part in parts], axis=0).reshape(-1, width)
    total = flat.astype(F32)
    for tile in range(TILES):
        span = slice(tile * step, (tile + 1) * step)
        inner = jnp.dot(flat, in_weight[:, span], preferred_element_type=F32)
        inner = (0.5 * inner * (1.0 + lax.erf(inner * (0.5**0.5)))).astype(BF16)
        total = total + jnp.dot(inner, back_weight[span, :], preferred_element_type=F32)
    return norm_rows(total, gain[...]).astype(BF16).reshape(-1, tokens, width)


def feed_first_kernel(gain, in_weight, back_weight, *rest):
    parts, out = rest[:-1], rest[-1]
    out[...] = feed_rows(parts, gain, in_weight, back_weight)


def feed_last_kernel(first_parts, last_parts, place, gain, match_weight, in_weight, back_weight, earlier, *rest):
    parts = rest[: len(last_parts)]
    merged, logits, done, first = rest[len(last_parts) :]
    slots = len(first_parts) * IMG_MOST
    done[:slots] = earlier[...]
    done[slots:] = feed_rows(parts, gain, in_weight, back_weight)
    for row in range(merged.shape[0]):
        slot = place[row]
        distance = slot // IMG_MOST
        spot = jnp.int32(0)
        for index, listed in enumerate(first_parts + last_parts):
            spot = jnp.where(distance == listed, index, spot)
        block = done[spot * IMG_MOST + slot % IMG_MOST]
        merged[row] = block
        first[row : row + 1, :] = block[0:1, :].astype(F32)
    logits[...] = lax.dot_general(
        match_weight[...], first[...].astype(BF16), (((1,), (1,)), ((), ())), preferred_element_type=F32
    )


def feed_cost(rows, width, inner_width):
    return pl.CostEstimate(
        flops=4 * rows * width * inner_width,
        bytes_accessed=4 * width * inner_width,
        transcendentals=rows * inner_width,
    )


def feed_first(parts, gain, in_weight, back_weight):
    count, tokens, width = parts[0].shape
    slots = len(parts) * count
    return pl.pallas_call(
        feed_first_kernel,
        out_shape=jax.ShapeDtypeStruct((slots, tokens, width), BF16),
        in_specs=[VMEM] * (3 + len(parts)),
        out_specs=VMEM,
        compiler_params=params(16),
        cost_estimate=feed_cost(slots * tokens, width, in_weight.shape[1]),
        name="feed_first",
    )(gain, in_weight, back_weight, *parts)


def feed_last(first_parts, last_parts, place, gain, match_weight, in_weight, back_weight, earlier, parts):
    count, tokens, width = parts[0].shape
    rows = place.shape[0]
    slots = (len(first_parts) + len(last_parts)) * count
    return pl.pallas_call(
        functools.partial(feed_last_kernel, first_parts, last_parts),
        out_shape=(
            jax.ShapeDtypeStruct((rows, tokens, width), BF16),
            jax.ShapeDtypeStruct((match_weight.shape[0], rows), F32),
        ),
        in_specs=[SMEM] + [VMEM] * (5 + len(parts)),
        out_specs=(VMEM, VMEM),
        scratch_shapes=[pltpu.VMEM((slots, tokens, width), BF16), pltpu.VMEM((rows, width), F32)],
        compiler_params=params(16),
        cost_estimate=feed_cost(len(parts) * count * tokens, width, in_weight.shape[1]),
        name="feed_last",
    )(place, gain, match_weight, in_weight, back_weight, earlier, *parts)


def body(
    pair_list,
    verify_order,
    image_slot,
    caption_slot,
    images,
    captions,
    query_weight,
    key_weight,
    value_weight,
    out_weight,
    gain_attn,
    in_weight,
    back_weight,
    gain_ffn,
    match_weight,
):
    img_count = lax.axis_size("img")
    cap_count = lax.axis_size("cap")
    far_steps = range(1, cap_count // CORES)
    half = img_count // 2
    chunks = tuple((img_count - 1 - index, index) for index in range(half))
    first_parts = sum(chunks[: half // 2], ())
    last_parts = sum(chunks[half // 2 :], ())

    def swap(array, axis, distance):
        size = lax.axis_size(axis)
        return lax.ppermute(array, axis, [(peer, peer ^ distance) for peer in range(size)])

    sibling = swap(captions, "cap", 1)
    table, place = make_table(
        pair_list.T, verify_order, image_slot, caption_slot, images.shape[0], img_count, cap_count
    )
    table = lax.all_to_all(table, ("img", "cap"), split_axis=0, concat_axis=0, tiled=True)
    keys = project_images(images, key_weight, True)
    value_weight, keys = lax.optimization_barrier((value_weight, keys))
    values = project_images(images, value_weight, False)
    pinned = pltpu.with_memory_space_constraint(captions, pltpu.HBM)
    far = [[] for _ in chunks]
    for step in far_steps:
        slots, *picked = pick_blocks(step, cap_count, chunks, table, pinned, sibling)
        for blocks, block in zip(far, picked):
            blocks.append(block)
    gain_attn = gain_attn.reshape(1, -1)
    gain_ffn = gain_ffn.reshape(1, -1)
    hidden = {}

    def after(value, parts):
        value, found = lax.optimization_barrier((value, [hidden[part] for part in parts]))
        hidden.update(zip(parts, found))
        return value

    def fetch(index):
        far[index] = [swap(block, "cap", step * CORES) for step, block in zip(far_steps, far[index])]

    fetch(0)
    far[1], keys = lax.optimization_barrier((far[1], keys))
    fetch(1)
    far[2:], values = lax.optimization_barrier((far[2:], values))
    for later in range(2, len(chunks)):
        fetch(later)
    for index, chunk in enumerate(chunks):
        if index >= 2:
            slots = after(slots, chunks[index - 2])
        blocks = attend(
            images.shape[1],
            chunk,
            slots,
            captions,
            sibling,
            far[index],
            keys,
            values,
            query_weight,
            out_weight,
            gain_attn,
        )
        for distance, block in zip(chunk, blocks):
            hidden[distance] = swap(block, "img", distance) if distance else block
    gain_ffn = after(gain_ffn, sum(chunks[:-1], ()))
    earlier = feed_first([hidden[part] for part in first_parts], gain_ffn, in_weight, back_weight)
    merged, logits = feed_last(
        first_parts,
        last_parts,
        place,
        gain_ffn,
        match_weight.T,
        in_weight,
        back_weight,
        earlier,
        [hidden[part] for part in last_parts],
    )
    return merged, logits.T


def solution(mesh):
    placed = (
        P(),
        P(("img", "cap")),
        P(),
        P(),
        P("img", None, None),
        P("cap", None, None),
        P(),
        P(),
        P(),
        P(),
        P(),
        P(),
        P(),
        P(),
        P(),
    )
    return jax.shard_map(
        body,
        mesh=mesh,
        in_specs=placed,
        out_specs=(P(("img", "cap"), None, None), P(("img", "cap"), None)),
        check_vma=False,
    )
```

```python
import functools

import jax
import jax.numpy as jnp
from jax import lax
from jax.experimental import pallas as pl
from jax.experimental.pallas import tpu as pltpu
from jax.sharding import PartitionSpec as P

HEADS = 12
IMG_MOST = 2
PIECES = 4
CORES = 2
PACK = 65536
KEY_PAD = 256
LANES = 128
GROUP = 256
F32 = jnp.float32
BF16 = jnp.bfloat16
SMALL = pl.CostEstimate(flops=1 << 16, bytes_accessed=1 << 10, transcendentals=0)

SMEM = pl.BlockSpec(memory_space=pltpu.SMEM)
VMEM = pl.BlockSpec(memory_space=pltpu.VMEM)
ANY = pl.BlockSpec(memory_space=pl.ANY)


def params(mib):
    return pltpu.CompilerParams(vmem_limit_bytes=mib * 1024 * 1024)


def norm_rows(hidden, gain):
    row_mean = jnp.mean(hidden, axis=-1, keepdims=True)
    centred = hidden - row_mean
    row_var = jnp.mean(centred * centred, axis=-1, keepdims=True)
    return centred * lax.rsqrt(row_var + 1e-06) * gain


def table_kernel(image_local, caption_count, pairs, order, image_slot, caption_slot, table, place, count):
    img_count = count.shape[0]
    me = lax.axis_index("img")
    for owner in range(img_count):
        count[owner] = 0
        for rank in range(IMG_MOST if img_count * IMG_MOST > order.shape[0] else 0):
            for column in range(caption_count):
                table[owner * caption_count + column, rank] = 0
    for row in range(order.shape[0]):
        pair = order[row]
        image = image_slot[pairs[0, pair]]
        caption = caption_slot[pairs[1, pair]]
        owner = image // image_local
        rank = count[owner]
        count[owner] = rank + 1
        entry = (image - owner * image_local) * PACK + caption
        for column in range(caption_count):
            table[owner * caption_count + column, rank] = entry
        place[row] = jnp.bitwise_xor(owner, me) * IMG_MOST + rank


def make_table(pairs, order, image_slot, caption_slot, image_local, img_count, caption_count):
    return pl.pallas_call(
        functools.partial(table_kernel, image_local, caption_count),
        out_shape=(
            jax.ShapeDtypeStruct((img_count * caption_count, LANES), jnp.int32),
            jax.ShapeDtypeStruct(order.shape, jnp.int32),
        ),
        in_specs=[SMEM] * 4,
        out_specs=(SMEM, SMEM),
        scratch_shapes=[pltpu.SMEM((img_count,), jnp.int32)],
        name="slot_table",
    )(pairs, order, image_slot, caption_slot)


def split_entry(entry, caption_local):
    caption = jnp.bitwise_and(entry, PACK - 1)
    owner = caption // caption_local
    return lax.shift_right_logical(entry, 16), owner, caption - owner * caption_local


def pick_kernel(step, cap_count, chunks, table, captions, sibling, slots, *rest):
    outs, own, sems = rest[: len(chunks)], rest[len(chunks)], rest[len(chunks) + 1]
    piece = own.shape[0] // PIECES
    copies = []
    for index in range(PIECES):
        span = pl.ds(index * piece, piece)
        copies.append(pltpu.make_async_copy(captions.at[span], own.at[span], sems.at[index]))
        copies[-1].start()
    me = lax.axis_index("img")
    mine = lax.axis_index("cap")
    asker = jnp.bitwise_xor(mine, step * CORES)
    picks = []
    for chunk, out in zip(chunks, outs):
        for index, distance in enumerate(chunk):
            verifier = jnp.bitwise_xor(me, distance) * cap_count
            for rank in range(IMG_MOST):
                slots[distance * IMG_MOST + rank] = table[verifier + mine, rank]
                _, owner, local = split_entry(table[verifier + asker, rank], own.shape[0])
                near = owner == jnp.bitwise_xor(mine, 1)
                picks.append((out, index * IMG_MOST + rank, near, local))

                @pl.when(near)
                def _():
                    out[index * IMG_MOST + rank] = sibling[local]

    for copy in copies:
        copy.wait()
    for out, spot, near, local in picks:

        @pl.when(jnp.logical_not(near))
        def _():
            out[spot] = own[local]


def pick_blocks(step, cap_count, chunks, table, own, sibling):
    slot_count = sum(len(chunk) for chunk in chunks) * IMG_MOST
    outs = tuple(
        jax.ShapeDtypeStruct((len(chunk) * IMG_MOST,) + own.shape[1:], own.dtype) for chunk in chunks
    )
    return pl.pallas_call(
        functools.partial(pick_kernel, step, cap_count, chunks),
        out_shape=(jax.ShapeDtypeStruct((slot_count,), jnp.int32),) + outs,
        in_specs=[SMEM, ANY, VMEM],
        out_specs=(SMEM,) + (VMEM,) * len(outs),
        scratch_shapes=[pltpu.VMEM(own.shape, own.dtype), pltpu.SemaphoreType.DMA((PIECES,))],
        compiler_params=params(8),
        cost_estimate=SMALL,
        name="pick_captions",
    )(table, own, sibling)


def project_kernel(turned, images, weight, out):
    count, rows, width = images.shape
    whole = rows // 16 * 16
    for image in range(count):
        found = jnp.dot(images[image], weight[...], preferred_element_type=F32).astype(BF16)
        if turned:
            out[image] = jnp.concatenate([found, jnp.zeros((KEY_PAD - rows, width), BF16)], axis=0).T
        else:
            out[image, whole:, :] = jnp.zeros((KEY_PAD - whole, width), BF16)
            out[image, :rows, :] = found


def project_images(images, weight, turned):
    count, rows, width = images.shape
    shape = (count, width, KEY_PAD) if turned else (count, KEY_PAD, width)
    return pl.pallas_call(
        functools.partial(project_kernel, turned),
        out_shape=jax.ShapeDtypeStruct(shape, BF16),
        in_specs=[VMEM] * 2,
        out_specs=VMEM,
        compiler_params=params(16),
        cost_estimate=SMALL,
        name="project_images",
    )(images, weight)


def attend_kernel(key_rows, far_count, chunk, slots, own, sibling, *rest):
    far = rest[:far_count]
    keys, values, query_weight, out_weight, gain = rest[far_count : far_count + 5]
    outs = rest[far_count + 5 : far_count + 5 + len(chunk)]
    rows, query, context = rest[far_count + 5 + len(chunk) :]
    column = lax.axis_index("cap")
    tokens, width = own.shape[1], own.shape[2]
    head_size = width // HEADS
    heads = GROUP // head_size
    pair_count = len(chunk) * IMG_MOST
    images = []
    for pair in range(pair_count):
        entry = slots[chunk[pair // IMG_MOST] * IMG_MOST + pair % IMG_MOST]
        image, owner, local = split_entry(entry, own.shape[0])
        images.append(image)
        apart = jnp.bitwise_xor(owner, column)

        @pl.when(apart == 0)
        def _():
            rows[pair] = own[local]

        @pl.when(apart == 1)
        def _():
            rows[pair] = sibling[local]

        for step in range(far_count):

            @pl.when(apart // CORES == step + 1)
            def _():
                rows[pair] = far[step][pair]

    flat = rows[...].reshape(pair_count * tokens, width)
    query[...] = jnp.dot(flat, query_weight[...], preferred_element_type=F32).astype(BF16)
    lane_head = lax.broadcasted_iota(jnp.int32, (tokens, GROUP), 1) // head_size
    visible = lax.broadcasted_iota(jnp.int32, (heads * tokens, KEY_PAD), 1) < key_rows
    scale = 1.0 / float(head_size) ** 0.5
    spans = [slice(group * GROUP, (group + 1) * GROUP) for group in range(width // GROUP)]

    def score(pair):
        found = []
        for span in spans:
            part = query[pair * tokens : (pair + 1) * tokens, span]
            stacked = jnp.concatenate(
                [jnp.where(lane_head == head, part, jnp.zeros_like(part)) for head in range(heads)],
                axis=0,
            )
            found.append(
                jnp.dot(stacked, keys[images[pair], span, :], preferred_element_type=F32)
            )
        return found

    def mix(pair, found):
        for span, scores in zip(spans, found):
            scores = jnp.where(visible, scores * scale, -jnp.inf)
            top = jnp.max(scores, axis=-1, keepdims=True)
            weights = jnp.exp(scores - top)
            share = 1.0 / jnp.sum(weights, axis=-1, keepdims=True)
            mixed = jnp.dot(
                weights.astype(BF16), values[images[pair], :, span], preferred_element_type=F32
            )
            mixed = mixed * share
            joined = mixed[:tokens]
            for head in range(1, heads):
                joined = jnp.where(lane_head == head, mixed[head * tokens : (head + 1) * tokens], joined)
            context[pair * tokens : (pair + 1) * tokens, span] = joined.astype(BF16)

    every = [score(pair) for pair in range(pair_count)]
    for pair in range(pair_count):
        mix(pair, every[pair])
    hidden = flat.astype(F32) + jnp.dot(context[...], out_weight[...], preferred_element_type=F32)
    hidden = norm_rows(hidden, gain[...]).astype(BF16).reshape(pair_count, tokens, width)
    for index, out in enumerate(outs):
        out[...] = hidden[index * IMG_MOST : (index + 1) * IMG_MOST]


def attend(key_rows, chunk, slots, own, sibling, far, keys, values, query_weight, out_weight, gain):
    tokens, width = own.shape[1:]
    pair_count = len(chunk) * IMG_MOST
    rows = pair_count * tokens
    return pl.pallas_call(
        functools.partial(attend_kernel, key_rows, len(far), chunk),
        out_shape=(jax.ShapeDtypeStruct((IMG_MOST, tokens, width), BF16),) * len(chunk),
        in_specs=[SMEM] + [VMEM] * (7 + len(far)),
        out_specs=(VMEM,) * len(chunk),
        scratch_shapes=[
            pltpu.VMEM((pair_count, tokens, width), BF16),
            pltpu.VMEM((rows, width), BF16),
            pltpu.VMEM((rows, width), BF16),
        ],
        compiler_params=params(16),
        cost_estimate=SMALL,
        name="attend",
    )(slots, own, sibling, *far, keys, values, query_weight, out_weight, gain)


TILES = 2


def feed_rows(parts, gain, in_weight, back_weight):
    count, tokens, width = parts[0].shape
    step = in_weight.shape[1] // TILES
    flat = jnp.concatenate([part[...] for part in parts], axis=0).reshape(-1, width)
    total = flat.astype(F32)
    for tile in range(TILES):
        span = slice(tile * step, (tile + 1) * step)
        inner = jnp.dot(flat, in_weight[:, span], preferred_element_type=F32)
        inner = (0.5 * inner * (1.0 + lax.erf(inner * (0.5**0.5)))).astype(BF16)
        total = total + jnp.dot(inner, back_weight[span, :], preferred_element_type=F32)
    return norm_rows(total, gain[...]).astype(BF16).reshape(-1, tokens, width)


def feed_first_kernel(gain, in_weight, back_weight, *rest):
    parts, out = rest[:-1], rest[-1]
    out[...] = feed_rows(parts, gain, in_weight, back_weight)


def feed_last_kernel(first_parts, last_parts, place, gain, match_weight, in_weight, back_weight, earlier, *rest):
    parts = rest[: len(last_parts)]
    merged, logits, done, first = rest[len(last_parts) :]
    slots = len(first_parts) * IMG_MOST
    done[:slots] = earlier[...]
    done[slots:] = feed_rows(parts, gain, in_weight, back_weight)
    for row in range(merged.shape[0]):
        slot = place[row]
        distance = slot // IMG_MOST
        spot = jnp.int32(0)
        for index, listed in enumerate(first_parts + last_parts):
            spot = jnp.where(distance == listed, index, spot)
        block = done[spot * IMG_MOST + slot % IMG_MOST]
        merged[row] = block
        first[row : row + 1, :] = block[0:1, :].astype(F32)
    logits[...] = lax.dot_general(
        match_weight[...], first[...].astype(BF16), (((1,), (1,)), ((), ())), preferred_element_type=F32
    )


def feed_cost(rows, width, inner_width):
    return pl.CostEstimate(
        flops=4 * rows * width * inner_width,
        bytes_accessed=4 * width * inner_width,
        transcendentals=rows * inner_width,
    )


def feed_first(parts, gain, in_weight, back_weight):
    count, tokens, width = parts[0].shape
    slots = len(parts) * count
    return pl.pallas_call(
        feed_first_kernel,
        out_shape=jax.ShapeDtypeStruct((slots, tokens, width), BF16),
        in_specs=[VMEM] * (3 + len(parts)),
        out_specs=VMEM,
        compiler_params=params(16),
        cost_estimate=feed_cost(slots * tokens, width, in_weight.shape[1]),
        name="feed_first",
    )(gain, in_weight, back_weight, *parts)


def feed_last(first_parts, last_parts, place, gain, match_weight, in_weight, back_weight, earlier, parts):
    count, tokens, width = parts[0].shape
    rows = place.shape[0]
    slots = (len(first_parts) + len(last_parts)) * count
    return pl.pallas_call(
        functools.partial(feed_last_kernel, first_parts, last_parts),
        out_shape=(
            jax.ShapeDtypeStruct((rows, tokens, width), BF16),
            jax.ShapeDtypeStruct((match_weight.shape[0], rows), F32),
        ),
        in_specs=[SMEM] + [VMEM] * (5 + len(parts)),
        out_specs=(VMEM, VMEM),
        scratch_shapes=[pltpu.VMEM((slots, tokens, width), BF16), pltpu.VMEM((rows, width), F32)],
        compiler_params=params(16),
        cost_estimate=feed_cost(len(parts) * count * tokens, width, in_weight.shape[1]),
        name="feed_last",
    )(place, gain, match_weight, in_weight, back_weight, earlier, *parts)


def body(
    pair_list,
    verify_order,
    image_slot,
    caption_slot,
    images,
    captions,
    query_weight,
    key_weight,
    value_weight,
    out_weight,
    gain_attn,
    in_weight,
    back_weight,
    gain_ffn,
    match_weight,
):
    img_count = lax.axis_size("img")
    cap_count = lax.axis_size("cap")
    far_steps = range(1, cap_count // CORES)
    half = img_count // 2
    chunks = tuple((img_count - 1 - index, index ^ 1) for index in range(half))
    first_parts = sum(chunks[: half // 2], ())
    last_parts = sum(chunks[half // 2 :], ())

    def swap(array, axis, distance):
        size = lax.axis_size(axis)
        return lax.ppermute(array, axis, [(peer, peer ^ distance) for peer in range(size)])

    sibling = swap(captions, "cap", 1)
    table, place = make_table(
        pair_list.T, verify_order, image_slot, caption_slot, images.shape[0], img_count, cap_count
    )
    table = lax.all_to_all(table, ("img", "cap"), split_axis=0, concat_axis=0, tiled=True)
    keys = project_images(images, key_weight, True)
    value_weight, keys = lax.optimization_barrier((value_weight, keys))
    values = project_images(images, value_weight, False)
    pinned = pltpu.with_memory_space_constraint(captions, pltpu.HBM)
    far = [[] for _ in chunks]
    for step in far_steps:
        slots, *picked = pick_blocks(step, cap_count, chunks, table, pinned, sibling)
        for blocks, block in zip(far, picked):
            blocks.append(block)
    gain_attn = gain_attn.reshape(1, -1)
    gain_ffn = gain_ffn.reshape(1, -1)
    hidden = {}

    def after(value, parts):
        value, found = lax.optimization_barrier((value, [hidden[part] for part in parts]))
        hidden.update(zip(parts, found))
        return value

    def fetch(index):
        far[index] = [swap(block, "cap", step * CORES) for step, block in zip(far_steps, far[index])]

    fetch(0)
    far[1], keys = lax.optimization_barrier((far[1], keys))
    fetch(1)
    far[2:], values = lax.optimization_barrier((far[2:], values))
    for later in range(2, len(chunks)):
        fetch(later)
    for index, chunk in enumerate(chunks):
        if index >= 2:
            slots = after(slots, chunks[index - 2])
        blocks = attend(
            images.shape[1],
            chunk,
            slots,
            captions,
            sibling,
            far[index],
            keys,
            values,
            query_weight,
            out_weight,
            gain_attn,
        )
        for distance, block in zip(chunk, blocks):
            hidden[distance] = swap(block, "img", distance) if distance else block
    gain_ffn = after(gain_ffn, sum(chunks[:-1], ()))
    earlier = feed_first([hidden[part] for part in first_parts], gain_ffn, in_weight, back_weight)
    merged, logits = feed_last(
        first_parts,
        last_parts,
        place,
        gain_ffn,
        match_weight.T,
        in_weight,
        back_weight,
        earlier,
        [hidden[part] for part in last_parts],
    )
    return merged, logits.T


def solution(mesh):
    placed = (
        P(),
        P(("img", "cap")),
        P(),
        P(),
        P("img", None, None),
        P("cap", None, None),
        P(),
        P(),
        P(),
        P(),
        P(),
        P(),
        P(),
        P(),
        P(),
    )
    return jax.shard_map(
        body,
        mesh=mesh,
        in_specs=placed,
        out_specs=(P(("img", "cap"), None, None), P(("img", "cap"), None)),
        check_vma=False,
    )
```

```python
import functools

import jax
import jax.numpy as jnp
from jax import lax
from jax.experimental import pallas as pl
from jax.experimental.pallas import tpu as pltpu
from jax.sharding import PartitionSpec as P

HEADS = 12
IMG_MOST = 2
PIECES = 4
CORES = 2
PACK = 65536
KEY_PAD = 256
LANES = 128
GROUP = 256
F32 = jnp.float32
BF16 = jnp.bfloat16
SMALL = pl.CostEstimate(flops=1 << 16, bytes_accessed=1 << 10, transcendentals=0)

SMEM = pl.BlockSpec(memory_space=pltpu.SMEM)
VMEM = pl.BlockSpec(memory_space=pltpu.VMEM)
ANY = pl.BlockSpec(memory_space=pl.ANY)


def params(mib):
    return pltpu.CompilerParams(vmem_limit_bytes=mib * 1024 * 1024)


def norm_rows(hidden, gain):
    row_mean = jnp.mean(hidden, axis=-1, keepdims=True)
    centred = hidden - row_mean
    row_var = jnp.mean(centred * centred, axis=-1, keepdims=True)
    return centred * lax.rsqrt(row_var + 1e-06) * gain


def table_kernel(image_local, caption_count, pairs, order, image_slot, caption_slot, table, place, count):
    img_count = count.shape[0]
    me = lax.axis_index("img")
    for owner in range(img_count):
        count[owner] = 0
        for rank in range(IMG_MOST if img_count * IMG_MOST > order.shape[0] else 0):
            for column in range(caption_count):
                table[owner * caption_count + column, rank] = 0
    for row in range(order.shape[0]):
        pair = order[row]
        image = image_slot[pairs[0, pair]]
        caption = caption_slot[pairs[1, pair]]
        owner = image // image_local
        rank = count[owner]
        count[owner] = rank + 1
        entry = (image - owner * image_local) * PACK + caption
        for column in range(caption_count):
            table[owner * caption_count + column, rank] = entry
        place[row] = jnp.bitwise_xor(owner, me) * IMG_MOST + rank


def make_table(pairs, order, image_slot, caption_slot, image_local, img_count, caption_count):
    return pl.pallas_call(
        functools.partial(table_kernel, image_local, caption_count),
        out_shape=(
            jax.ShapeDtypeStruct((img_count * caption_count, LANES), jnp.int32),
            jax.ShapeDtypeStruct(order.shape, jnp.int32),
        ),
        in_specs=[SMEM] * 4,
        out_specs=(SMEM, SMEM),
        scratch_shapes=[pltpu.SMEM((img_count,), jnp.int32)],
        name="slot_table",
    )(pairs, order, image_slot, caption_slot)


def split_entry(entry, caption_local):
    caption = jnp.bitwise_and(entry, PACK - 1)
    owner = caption // caption_local
    return lax.shift_right_logical(entry, 16), owner, caption - owner * caption_local


def pick_kernel(step, cap_count, chunks, table, captions, sibling, slots, *rest):
    outs, own, sems = rest[: len(chunks)], rest[len(chunks)], rest[len(chunks) + 1]
    piece = own.shape[0] // PIECES
    copies = []
    for index in range(PIECES):
        span = pl.ds(index * piece, piece)
        copies.append(pltpu.make_async_copy(captions.at[span], own.at[span], sems.at[index]))
        copies[-1].start()
    me = lax.axis_index("img")
    mine = lax.axis_index("cap")
    asker = jnp.bitwise_xor(mine, step * CORES)
    picks = []
    for chunk, out in zip(chunks, outs):
        for index, distance in enumerate(chunk):
            verifier = jnp.bitwise_xor(me, distance) * cap_count
            for rank in range(IMG_MOST):
                slots[distance * IMG_MOST + rank] = table[verifier + mine, rank]
                _, owner, local = split_entry(table[verifier + asker, rank], own.shape[0])
                near = owner == jnp.bitwise_xor(mine, 1)
                picks.append((out, index * IMG_MOST + rank, near, local))

                @pl.when(near)
                def _():
                    out[index * IMG_MOST + rank] = sibling[local]

    for copy in copies:
        copy.wait()
    for out, spot, near, local in picks:

        @pl.when(jnp.logical_not(near))
        def _():
            out[spot] = own[local]


def pick_blocks(step, cap_count, chunks, table, own, sibling):
    slot_count = sum(len(chunk) for chunk in chunks) * IMG_MOST
    outs = tuple(
        jax.ShapeDtypeStruct((len(chunk) * IMG_MOST,) + own.shape[1:], own.dtype) for chunk in chunks
    )
    return pl.pallas_call(
        functools.partial(pick_kernel, step, cap_count, chunks),
        out_shape=(jax.ShapeDtypeStruct((slot_count,), jnp.int32),) + outs,
        in_specs=[SMEM, ANY, VMEM],
        out_specs=(SMEM,) + (VMEM,) * len(outs),
        scratch_shapes=[pltpu.VMEM(own.shape, own.dtype), pltpu.SemaphoreType.DMA((PIECES,))],
        compiler_params=params(8),
        cost_estimate=SMALL,
        name="pick_captions",
    )(table, own, sibling)


def project_kernel(turned, images, weight, out):
    count, rows, width = images.shape
    whole = rows // 16 * 16
    for image in range(count):
        found = jnp.dot(images[image], weight[...], preferred_element_type=F32).astype(BF16)
        if turned:
            out[image] = jnp.concatenate([found, jnp.zeros((KEY_PAD - rows, width), BF16)], axis=0).T
        else:
            out[image, whole:, :] = jnp.zeros((KEY_PAD - whole, width), BF16)
            out[image, :rows, :] = found


def project_images(images, weight, turned):
    count, rows, width = images.shape
    shape = (count, width, KEY_PAD) if turned else (count, KEY_PAD, width)
    return pl.pallas_call(
        functools.partial(project_kernel, turned),
        out_shape=jax.ShapeDtypeStruct(shape, BF16),
        in_specs=[VMEM] * 2,
        out_specs=VMEM,
        compiler_params=params(16),
        cost_estimate=SMALL,
        name="project_images",
    )(images, weight)


def attend_kernel(key_rows, far_count, chunk, slots, own, sibling, *rest):
    far = rest[:far_count]
    keys, values, query_weight, out_weight, gain = rest[far_count : far_count + 5]
    outs = rest[far_count + 5 : far_count + 5 + len(chunk)]
    rows, query, context = rest[far_count + 5 + len(chunk) :]
    column = lax.axis_index("cap")
    tokens, width = own.shape[1], own.shape[2]
    head_size = width // HEADS
    heads = GROUP // head_size
    pair_count = len(chunk) * IMG_MOST
    images = []
    for pair in range(pair_count):
        entry = slots[chunk[pair // IMG_MOST] * IMG_MOST + pair % IMG_MOST]
        image, owner, local = split_entry(entry, own.shape[0])
        images.append(image)
        apart = jnp.bitwise_xor(owner, column)

        @pl.when(apart == 0)
        def _():
            rows[pair] = own[local]

        @pl.when(apart == 1)
        def _():
            rows[pair] = sibling[local]

        for step in range(far_count):

            @pl.when(apart // CORES == step + 1)
            def _():
                rows[pair] = far[step][pair]

    flat = rows[...].reshape(pair_count * tokens, width)
    query[...] = jnp.dot(flat, query_weight[...], preferred_element_type=F32).astype(BF16)
    lane_head = lax.broadcasted_iota(jnp.int32, (tokens, GROUP), 1) // head_size
    visible = lax.broadcasted_iota(jnp.int32, (heads * tokens, KEY_PAD), 1) < key_rows
    scale = 1.0 / float(head_size) ** 0.5
    spans = [slice(group * GROUP, (group + 1) * GROUP) for group in range(width // GROUP)]

    def score(pair):
        found = []
        for span in spans:
            part = query[pair * tokens : (pair + 1) * tokens, span]
            stacked = jnp.concatenate(
                [jnp.where(lane_head == head, part, jnp.zeros_like(part)) for head in range(heads)],
                axis=0,
            )
            found.append(
                jnp.dot(stacked, keys[images[pair], span, :], preferred_element_type=F32)
            )
        return found

    def mix(pair, found):
        for span, scores in zip(spans, found):
            scores = jnp.where(visible, scores * scale, -jnp.inf)
            top = jnp.max(scores, axis=-1, keepdims=True)
            weights = jnp.exp(scores - top)
            share = 1.0 / jnp.sum(weights, axis=-1, keepdims=True)
            mixed = jnp.dot(
                weights.astype(BF16), values[images[pair], :, span], preferred_element_type=F32
            )
            mixed = mixed * share
            joined = mixed[:tokens]
            for head in range(1, heads):
                joined = jnp.where(lane_head == head, mixed[head * tokens : (head + 1) * tokens], joined)
            context[pair * tokens : (pair + 1) * tokens, span] = joined.astype(BF16)

    every = [score(pair) for pair in range(pair_count)]
    for pair in range(pair_count):
        mix(pair, every[pair])
    hidden = flat.astype(F32) + jnp.dot(context[...], out_weight[...], preferred_element_type=F32)
    hidden = norm_rows(hidden, gain[...]).astype(BF16).reshape(pair_count, tokens, width)
    for index, out in enumerate(outs):
        out[...] = hidden[index * IMG_MOST : (index + 1) * IMG_MOST]


def attend(key_rows, chunk, slots, own, sibling, far, keys, values, query_weight, out_weight, gain):
    tokens, width = own.shape[1:]
    pair_count = len(chunk) * IMG_MOST
    rows = pair_count * tokens
    return pl.pallas_call(
        functools.partial(attend_kernel, key_rows, len(far), chunk),
        out_shape=(jax.ShapeDtypeStruct((IMG_MOST, tokens, width), BF16),) * len(chunk),
        in_specs=[SMEM] + [VMEM] * (7 + len(far)),
        out_specs=(VMEM,) * len(chunk),
        scratch_shapes=[
            pltpu.VMEM((pair_count, tokens, width), BF16),
            pltpu.VMEM((rows, width), BF16),
            pltpu.VMEM((rows, width), BF16),
        ],
        compiler_params=params(16),
        cost_estimate=SMALL,
        name="attend",
    )(slots, own, sibling, *far, keys, values, query_weight, out_weight, gain)


TILES = 2


def feed_rows(parts, gain, in_weight, back_weight):
    count, tokens, width = parts[0].shape
    step = in_weight.shape[1] // TILES
    flat = jnp.concatenate([part[...] for part in parts], axis=0).reshape(-1, width)
    total = flat.astype(F32)
    for tile in range(TILES):
        span = slice(tile * step, (tile + 1) * step)
        inner = jnp.dot(flat, in_weight[:, span], preferred_element_type=F32)
        inner = (0.5 * inner * (1.0 + lax.erf(inner * (0.5**0.5)))).astype(BF16)
        total = total + jnp.dot(inner, back_weight[span, :], preferred_element_type=F32)
    return norm_rows(total, gain[...]).astype(BF16).reshape(-1, tokens, width)


def feed_first_kernel(gain, in_weight, back_weight, *rest):
    parts, out = rest[:-1], rest[-1]
    out[...] = feed_rows(parts, gain, in_weight, back_weight)


def feed_last_kernel(first_parts, last_parts, place, gain, match_weight, in_weight, back_weight, earlier, *rest):
    parts = rest[: len(last_parts)]
    merged, logits, done, first = rest[len(last_parts) :]
    slots = len(first_parts) * IMG_MOST
    done[:slots] = earlier[...]
    done[slots:] = feed_rows(parts, gain, in_weight, back_weight)
    for row in range(merged.shape[0]):
        slot = place[row]
        distance = slot // IMG_MOST
        spot = jnp.int32(0)
        for index, listed in enumerate(first_parts + last_parts):
            spot = jnp.where(distance == listed, index, spot)
        block = done[spot * IMG_MOST + slot % IMG_MOST]
        merged[row] = block
        first[row : row + 1, :] = block[0:1, :].astype(F32)
    logits[...] = lax.dot_general(
        match_weight[...], first[...].astype(BF16), (((1,), (1,)), ((), ())), preferred_element_type=F32
    )


def feed_cost(rows, width, inner_width):
    return pl.CostEstimate(
        flops=4 * rows * width * inner_width,
        bytes_accessed=4 * width * inner_width,
        transcendentals=rows * inner_width,
    )


def feed_first(parts, gain, in_weight, back_weight):
    count, tokens, width = parts[0].shape
    slots = len(parts) * count
    return pl.pallas_call(
        feed_first_kernel,
        out_shape=jax.ShapeDtypeStruct((slots, tokens, width), BF16),
        in_specs=[VMEM] * (3 + len(parts)),
        out_specs=VMEM,
        compiler_params=params(16),
        cost_estimate=feed_cost(slots * tokens, width, in_weight.shape[1]),
        name="feed_first",
    )(gain, in_weight, back_weight, *parts)


def feed_last(first_parts, last_parts, place, gain, match_weight, in_weight, back_weight, earlier, parts):
    count, tokens, width = parts[0].shape
    rows = place.shape[0]
    slots = (len(first_parts) + len(last_parts)) * count
    return pl.pallas_call(
        functools.partial(feed_last_kernel, first_parts, last_parts),
        out_shape=(
            jax.ShapeDtypeStruct((rows, tokens, width), BF16),
            jax.ShapeDtypeStruct((match_weight.shape[0], rows), F32),
        ),
        in_specs=[SMEM] + [VMEM] * (5 + len(parts)),
        out_specs=(VMEM, VMEM),
        scratch_shapes=[pltpu.VMEM((slots, tokens, width), BF16), pltpu.VMEM((rows, width), F32)],
        compiler_params=params(16),
        cost_estimate=feed_cost(len(parts) * count * tokens, width, in_weight.shape[1]),
        name="feed_last",
    )(place, gain, match_weight, in_weight, back_weight, earlier, *parts)


def body(
    pair_list,
    verify_order,
    image_slot,
    caption_slot,
    images,
    captions,
    query_weight,
    key_weight,
    value_weight,
    out_weight,
    gain_attn,
    in_weight,
    back_weight,
    gain_ffn,
    match_weight,
):
    img_count = lax.axis_size("img")
    cap_count = lax.axis_size("cap")
    far_steps = range(1, cap_count // CORES)
    half = img_count // 2
    chunks = tuple((img_count - 1 - (index ^ 1), index ^ 1) for index in range(half))
    first_parts = sum(chunks[: half // 2], ())
    last_parts = sum(chunks[half // 2 :], ())

    def swap(array, axis, distance):
        size = lax.axis_size(axis)
        return lax.ppermute(array, axis, [(peer, peer ^ distance) for peer in range(size)])

    sibling = swap(captions, "cap", 1)
    table, place = make_table(
        pair_list.T, verify_order, image_slot, caption_slot, images.shape[0], img_count, cap_count
    )
    table = lax.all_to_all(table, ("img", "cap"), split_axis=0, concat_axis=0, tiled=True)
    keys = project_images(images, key_weight, True)
    value_weight, keys = lax.optimization_barrier((value_weight, keys))
    values = project_images(images, value_weight, False)
    pinned = pltpu.with_memory_space_constraint(captions, pltpu.HBM)
    far = [[] for _ in chunks]
    for step in far_steps:
        slots, *picked = pick_blocks(step, cap_count, chunks, table, pinned, sibling)
        for blocks, block in zip(far, picked):
            blocks.append(block)
    gain_attn = gain_attn.reshape(1, -1)
    gain_ffn = gain_ffn.reshape(1, -1)
    hidden = {}

    def after(value, parts):
        value, found = lax.optimization_barrier((value, [hidden[part] for part in parts]))
        hidden.update(zip(parts, found))
        return value

    def fetch(index):
        far[index] = [swap(block, "cap", step * CORES) for step, block in zip(far_steps, far[index])]

    fetch(0)
    far[1], keys = lax.optimization_barrier((far[1], keys))
    fetch(1)
    far[2:], values = lax.optimization_barrier((far[2:], values))
    for later in range(2, len(chunks)):
        fetch(later)
    for index, chunk in enumerate(chunks):
        if index >= 2:
            slots = after(slots, chunks[index - 2])
        blocks = attend(
            images.shape[1],
            chunk,
            slots,
            captions,
            sibling,
            far[index],
            keys,
            values,
            query_weight,
            out_weight,
            gain_attn,
        )
        for distance, block in zip(chunk, blocks):
            hidden[distance] = swap(block, "img", distance) if distance else block
    gain_ffn = after(gain_ffn, sum(chunks[:-1], ()))
    earlier = feed_first([hidden[part] for part in first_parts], gain_ffn, in_weight, back_weight)
    merged, logits = feed_last(
        first_parts,
        last_parts,
        place,
        gain_ffn,
        match_weight.T,
        in_weight,
        back_weight,
        earlier,
        [hidden[part] for part in last_parts],
    )
    return merged, logits.T


def solution(mesh):
    placed = (
        P(),
        P(("img", "cap")),
        P(),
        P(),
        P("img", None, None),
        P("cap", None, None),
        P(),
        P(),
        P(),
        P(),
        P(),
        P(),
        P(),
        P(),
        P(),
    )
    return jax.shard_map(
        body,
        mesh=mesh,
        in_specs=placed,
        out_specs=(P(("img", "cap"), None, None), P(("img", "cap"), None)),
        check_vma=False,
    )
```
